32 devices in a mesh: dp: 8 (over z, y), tensor: 4 (over x, core).
Axes of the slice: x: 2, y: 2, z: 4, core: 2. Of those that a mesh axis runs over, the one named last changes fastest.
Arguments:
- inputs: bfloat16 [12288, 768], P(('dp', 'tensor')), may hold values from -6 to 6
- segments: int32 [12288], P('dp'), may hold values from 0 to 8, as said below
- first_gain: bfloat16 [768], replicated, may hold values from 0.25 to 1.75
- query_weight: bfloat16 [768, 768], P(None, 'tensor'), may hold values from -0.078125 to 0.078125
- lookup_projection: bfloat16 [768, 768], P(None, 'tensor'), may hold values from -0.078125 to 0.078125
- value_weight: bfloat16 [768, 768], P(None, 'tensor'), may hold values from -0.21875 to 0.21875
- output_weight: bfloat16 [768, 768], P('tensor'), may hold values from -1.75 to 1.75
- bucket_bias_table: bfloat16 [32, 12], P(None, 'tensor'), may hold values from -4 to 4
- second_gain: bfloat16 [768], replicated, may hold values from 0.25 to 1.75
- inner_weight: bfloat16 [768, 3072], P(None, 'tensor'), may hold values from -0.21875 to 0.21875
- outer_weight: bfloat16 [3072, 768], P('tensor'), may hold values from -0.15625 to 0.15625
- cotangent: bfloat16 [12288, 768], P(('dp', 'tensor')), may hold values from -6 to 6
Outputs:
- layer_output: bfloat16 [12288, 768], P(('dp', 'tensor'))
- input_grad: float32 [12288, 768], P(('dp', 'tensor'))
- query_weight_grad: float32 [768, 768], P(None, 'tensor')
- key_weight_grad: float32 [768, 768], P(None, 'tensor')
- content_projection_adjoint: float32 [768, 768], P(None, 'tensor')
- output_weight_grad: float32 [768, 768], P('tensor')
- table_grad: float32 [32, 12], P(None, 'tensor')
- inner_weight_grad: float32 [768, 3072], P(None, 'tensor')
- outer_weight_grad: float32 [3072, 768], P('tensor')
- gain_grads: float32 [2, 768], replicated
The draws below stay inside these ranges and needn't reach their ends.
Inputs may be any that keep to these rules, and one draw needn't show every extreme that they name: `segments`: each block of 1536 tokens holds whole sequences numbered 0, 1, 2, ... in order; the first has exactly 1024 tokens, the others are multiples of 64 tokens and at most 1024; in some block every sequence after the first has 64 tokens.
All inputs are finite; a program needn't handle non-finite values.
Results may differ from the reference program's by a relative error of at most 0.015.
Values may be sent and summed in bfloat16 or wider, within the bound.
No kernel may reach another device: no remote copies, remote signals or barrier semaphores. Data moves between devices by JAX's collectives and lax.ppermute only.
A program may use at most 128 MiB of HBM per device.

```python
import jax
import jax.numpy as jnp
from jax import lax

D = 768
HEADS = 12
DH = 64
FF = 3072
BUCKETS = 32
LONGEST_SPAN = 1024
TOK_DEV = 1536
TOKENS = 12288
N_DP = 8


def draw_segments(key, part):
    cell_width = max(LONGEST_SPAN // 16, 1)
    cell_count = TOK_DEV // cell_width
    long_cells = LONGEST_SPAN // cell_width
    blocks = TOKENS // TOK_DEV
    cell_index = jnp.arange(cell_count, dtype=jnp.int32)[None, :]
    block_index = jnp.arange(blocks, dtype=jnp.int32)[:, None]
    coin_draws = jax.random.randint(key, (blocks, cell_count), 0, 4)
    beyond = cell_index - long_cells
    later = cell_index >= long_cells
    starts = (cell_index == 0) | later & ((coin_draws == 0) | (beyond % long_cells == 0) | (block_index == 0))
    numbers = jnp.cumsum(starts.astype(jnp.int32), axis=1) - 1
    return jnp.repeat(numbers, cell_width, axis=1).reshape(TOKENS).astype(jnp.int32)


def steps_of(key, shape, shards, least, high):
    factor_of = 1.0
    for dim, shards_of in shards:
        draws = jax.random.uniform(jax.random.fold_in(jax.random.fold_in(key, 6), dim), (shards_of,), jnp.float32, least / len(shards), high / len(shards))
        factor_of = factor_of * jnp.repeat(jnp.exp(draws), shape[dim] // shards_of).reshape((-1,) + (1,) * (len(shape) - 1 - dim))
    return factor_of


def normal_values(key, extent, deviation, most, pieces=(), held_as=jnp.bfloat16):
    array = deviation * jax.random.normal(key, extent, jnp.float32)
    if pieces:
        array = array * steps_of(key, extent, pieces, -0.22, 0.18)
    return jnp.clip(array, -most, most).astype(held_as)


def setup_inputs(seed: int = 0) -> dict:
    splits = jax.random.split(jax.random.key(seed), 13)
    inputs = normal_values(splits[0], (TOKENS, D), 1.0, 6.0, ((0, 32),))
    segments = draw_segments(jax.random.fold_in(splits[12], 71), 0)
    first_gain = jnp.clip(1.0 + 0.15 * jax.random.normal(splits[2], (D,), jnp.float32), 0.25, 1.75).astype(jnp.bfloat16)
    query_weight = normal_values(splits[3], (D, HEADS * DH), (8 * D) ** -0.5, 0.078125, ((1, 4),))
    lookup_projection = normal_values(splits[4], (D, HEADS * DH), (8 * D) ** -0.5, 0.078125, ((1, 4),))
    value_weight = normal_values(splits[5], (D, HEADS * DH), D ** -0.5, 0.21875, ((1, 4),))
    output_weight = normal_values(splits[6], (HEADS * DH, D), (HEADS * DH // 64) ** -0.5, 1.75, ((0, 4),))
    bucket_bias_table = normal_values(splits[7], (BUCKETS, HEADS), 1.0, 4.0, ((1, 4),))
    second_gain = jnp.clip(1.0 + 0.15 * jax.random.normal(splits[8], (D,), jnp.float32), 0.25, 1.75).astype(jnp.bfloat16)
    inner_weight = normal_values(splits[9], (D, FF), D ** -0.5, 0.21875, ((1, 4),))
    outer_weight = normal_values(splits[10], (FF, D), (FF // 2) ** -0.5, 0.15625, ((0, 4),))
    cotangent = normal_values(splits[11], (TOKENS, D), 1.0, 6.0, ((0, 32),))
    return {"inputs": inputs, "segments": segments, "first_gain": first_gain, "query_weight": query_weight, "lookup_projection": lookup_projection, "value_weight": value_weight, "output_weight": output_weight, "bucket_bias_table": bucket_bias_table, "second_gain": second_gain, "inner_weight": inner_weight, "outer_weight": outer_weight, "cotangent": cotangent}


@jax.custom_vjp
def low(v):
    return lax.optimization_barrier(v.astype(jnp.bfloat16)).astype(jnp.float32)

@jax.custom_vjp
def low_back(v):
    return v

def low_keep(v):
    return (low(v), None)

def low_pass(kept, grad):
    return (grad,)

def back_keep(v):
    return (v, None)

def back_low(kept, grad):
    return (low(grad),)
low.defvjp(low_keep, low_pass)
low_back.defvjp(back_keep, back_low)
EDGES = (8, 12, 16, 23, 32, 46, 64, 91)
EPSILON = 1e-06
MASKED = -1000000000.0

def buckets_of(offset):
    distance = jnp.abs(offset)
    coarse = jnp.full(distance.shape, 7, jnp.int32)
    for boundary in EDGES:
        coarse = coarse + (distance >= boundary).astype(jnp.int32)
    bucket = jnp.where(distance < 8, distance, coarse)
    return (bucket + jnp.where(offset > 0, 16, 0)).astype(jnp.int32)

def matmul(left, right):
    return jnp.dot(left, right, precision=lax.Precision.HIGHEST)

def root_norm(values, gains):
    return values * lax.rsqrt(lax.optimization_barrier(jnp.mean(values * values, axis=-1, keepdims=True)) + EPSILON) * gains

def smooth_gate(values):
    return jax.nn.gelu(values, approximate=True)

def bias_of(column, bucket_ids):
    total = jnp.zeros(bucket_ids.shape, column.dtype)
    for slot in range(BUCKETS):
        total = total + jnp.where(bucket_ids == slot, column[slot], jnp.zeros((), column.dtype))
    return total

def head_attention(queries, key_rows, value_rows, column, bucket_ids, visible_pairs_flag):
    raw_scores = matmul(queries, key_rows.T) + bias_of(column, bucket_ids)
    masked_fill = jnp.full(raw_scores.shape, MASKED, raw_scores.dtype)
    scores = jnp.where(visible_pairs_flag, low_back(raw_scores), masked_fill)
    probability = jax.nn.softmax(scores, axis=-1)
    return matmul(low(probability), value_rows)

def block_forward(params, inputs, bucket_ids, visible_pairs_flag):
    first_gain, query_weight, lookup_projection, value_weight, output_weight, bucket_bias_table, second_gain, inner_weight, outer_weight = params
    normed = low(root_norm(inputs, first_gain))

    def project(weight):
        projected = low_back(low(matmul(normed, weight)))
        return projected.reshape(inputs.shape[0], HEADS, DH).transpose(1, 0, 2)
    queries = project(query_weight)
    key_rows = project(lookup_projection)
    value_rows = project(value_weight)

    def one_head(head_item):
        return head_attention(head_item[0], head_item[1], head_item[2], head_item[3], bucket_ids, visible_pairs_flag)
    context = lax.map(jax.checkpoint(one_head), (queries, key_rows, value_rows, bucket_bias_table.T))
    context = low_back(low(context.transpose(1, 0, 2).reshape(inputs.shape[0], HEADS * DH)))
    attended = low_back(matmul(context, output_weight))
    middle = inputs + attended
    normed_two = low(root_norm(middle, second_gain))
    inner_value = low_back(matmul(normed_two, inner_weight))
    hidden = low(smooth_gate(inner_value))
    return middle + low_back(matmul(hidden, outer_weight))

def add_pair(left_term, right_term):
    return left_term + right_term

def reference(inputs, segments, first_gain, query_weight, lookup_projection, value_weight, output_weight, bucket_bias_table, second_gain, inner_weight, outer_weight, cotangent):
    params = tuple((weight.astype(jnp.float32) for weight in (first_gain, query_weight, lookup_projection, value_weight, output_weight, bucket_bias_table, second_gain, inner_weight, outer_weight)))
    position = jnp.arange(TOK_DEV, dtype=jnp.int32)
    bucket_ids = buckets_of(position[None, :] - position[:, None])
    blocks_in = inputs.astype(jnp.float32).reshape(N_DP, TOK_DEV, D)
    blocks_seg = segments.astype(jnp.int32).reshape(N_DP, TOK_DEV)
    blocks_cot = cotangent.astype(jnp.float32).reshape(N_DP, TOK_DEV, D)

    def per_block(totals, block_item):
        block_in, block_seg, block_cot = block_item
        visible_pairs_flag = block_seg[:, None] == block_seg[None, :]

        def forward(weights, values):
            return block_forward(weights, values, bucket_ids, visible_pairs_flag)
        result, pullback = jax.vjp(forward, params, block_in)
        gradients, input_part = pullback(block_cot.astype(result.dtype))
        return (jax.tree.map(add_pair, totals, gradients), (result.astype(jnp.bfloat16), input_part))
    initial = jax.tree.map(jnp.zeros_like, params)
    totals, (outputs, input_grad) = lax.scan(per_block, initial, (blocks_in, blocks_seg, blocks_cot))
    factor = float(TOKENS) ** (-0.5)
    gain_one_grad, query_grad, key_grad, value_grad, output_grad, table_grad, gain_two_grad, inner_grad, outer_grad = totals
    gain_grads = jnp.stack([gain_one_grad, gain_two_grad]) * factor
    return (outputs.reshape(TOKENS, D), input_grad.reshape(TOKENS, D), query_grad * factor, key_grad * factor, value_grad * factor, output_grad * factor, table_grad * factor, inner_grad * factor, outer_grad * factor, gain_grads)
```

```python
import functools

import jax
import jax.numpy as jnp
from jax import lax
from jax.experimental import pallas as pl
from jax.experimental.pallas import tpu as pltpu
from jax.sharding import PartitionSpec as P

DH = 64
LONG = 1024
QT = 256
NEAR = 128
WIDE = 768
EDGES = (8, 12, 16, 23, 32, 46, 64, 91)
EPSILON = 1e-06
MASKED = -1000000000.0
BF = jnp.bfloat16
F32 = jnp.float32


def buckets_of(offset):
    distance = jnp.abs(offset)
    coarse = jnp.full(distance.shape, 7, jnp.int32)
    for boundary in EDGES:
        coarse = coarse + (distance >= boundary).astype(jnp.int32)
    bucket = jnp.where(distance < 8, distance, coarse)
    return bucket + jnp.where(offset > 0, 16, 0).astype(jnp.int32)


def dot(left, right, dims=((1,), (0,))):
    return lax.dot_general(left, right, (dims, ((), ())), preferred_element_type=F32)


ROWS_T = ((1,), (1,))
T_ROWS = ((0,), (0,))


def params(limit=56):
    return pltpu.CompilerParams(vmem_limit_bytes=limit * 1024 * 1024)


def vmem():
    return pl.BlockSpec(memory_space=pltpu.VMEM)


def smem():
    return pl.BlockSpec(memory_space=pltpu.SMEM)


def near_kernel(table_ref, near_ref):
    head_count = near_ref.shape[0]
    lane = lax.broadcasted_iota(jnp.int32, (8, WIDE), 1)
    bucket = buckets_of(lane - (QT + NEAR - 1))
    for head in range(head_count):
        line = jnp.zeros((8, WIDE), F32)
        for slot in range(table_ref.shape[0]):
            line = jnp.where(bucket == slot, table_ref[slot, head], line)
        rows = jnp.broadcast_to(line[:1], (QT, WIDE))
        turned = pltpu.roll(rows, WIDE - QT + 1, 1, stride=1, stride_axis=0)
        near_ref[head] = turned[:, : QT + 2 * NEAR]


def near_bias(table):
    head_count = table.shape[1]
    return pl.pallas_call(
        near_kernel,
        out_shape=jax.ShapeDtypeStruct((head_count, QT, QT + 2 * NEAR), F32),
        in_specs=[smem()],
        out_specs=vmem(),
        compiler_params=params(),
        name="near_bias",
    )(table)


def pieces_of(tile, keys):
    low = max(tile * QT - NEAR, 0)
    high = min(tile * QT + QT + NEAR, keys)
    return low, high, low - (tile * QT - NEAR)


def forward_kernel(
    place_ref,
    table_ref,
    block0,
    block1,
    block2,
    block3,
    weight_ref,
    near_ref,
    row_segment_ref,
    key_segment_ref,
    output_weight_ref,
    query_ref,
    key_ref,
    value_ref,
    prob_ref,
    rest_ref,
    context_ref,
    attended_ref,
    gathered,
):
    head = pl.program_id(0)
    head_count = pl.num_programs(0)
    place = place_ref[0]
    blocks = (block0, block1, block2, block3)
    size = block0.shape[0]
    for step, block in enumerate(blocks):
        row = pl.multiple_of((place ^ step) * size, size)
        made = dot(block[...], weight_ref[0]).astype(BF)
        query_ref[0, pl.ds(row, size), :] = made[:, :DH]
        key_ref[0, pl.ds(row, size), :] = made[:, DH : 2 * DH]
        value_ref[0, pl.ds(row, size), :] = made[:, 2 * DH :]
    total = query_ref.shape[1]
    left_bias = table_ref[15, head]
    right_bias = table_ref[31, head]

    def tiles(first, keys, store_ref, masked):
        for tile in range(keys // QT):
            low, high, lane = pieces_of(tile, keys)
            rows = slice(first + tile * QT, first + tile * QT + QT)
            scores = dot(query_ref[0, rows, :], key_ref[0, first : first + keys, :], ROWS_T)
            parts = []
            if low > 0:
                parts.append((0, low, scores[:, :low] + left_bias))
            parts.append((low, high, scores[:, low:high] + near_ref[0, :, lane : lane + high - low]))
            if high < keys:
                parts.append((high, keys, scores[:, high:] + right_bias))
            if masked:
                row_segment = row_segment_ref[tile * QT : tile * QT + QT, :]
                parts = [
                    (a, b, jnp.where(row_segment == key_segment_ref[:, a:b], part, MASKED))
                    for a, b, part in parts
                ]
            peak = functools.reduce(
                jnp.maximum, [jnp.max(part, axis=1, keepdims=True) for a, b, part in parts]
            )
            parts = [(a, b, jnp.exp(part - peak)) for a, b, part in parts]
            whole = sum(jnp.sum(part, axis=1, keepdims=True) for a, b, part in parts)
            share = 1.0 / whole
            for a, b, part in parts:
                store_ref[0, tile * QT : tile * QT + QT, a:b] = (part * share).astype(BF)
            context_ref[0, rows, :] = dot(
                store_ref[0, tile * QT : tile * QT + QT, :], value_ref[0, first : first + keys, :]
            ).astype(BF)

    tiles(0, LONG, prob_ref, False)
    if total > LONG:
        tiles(LONG, total - LONG, rest_ref, True)
    for which in range(gathered.shape[1] // DH):

        @pl.when(head == which)
        def _():
            gathered[:, which * DH : which * DH + DH] = context_ref[0]

    @pl.when(head == head_count - 1)
    def _():
        for step in range(4):
            row = pl.multiple_of((place ^ step) * size, size)
            attended_ref[step] = dot(
                gathered[pl.ds(row, size), :], output_weight_ref[...]
            ).astype(BF)


def attend_forward(place, table, blocks, weights, near, row_segment, key_segment, output_weight):
    head_count, width, _ = weights.shape
    size = blocks[0].shape[0]
    total = 4 * size
    rest = total - LONG
    by_head = lambda *shape: pl.BlockSpec((1, *shape), lambda h: (h, *(0 for _ in shape)))
    whole = lambda *shape: pl.BlockSpec(shape, lambda h: tuple(0 for _ in shape))
    struct = jax.ShapeDtypeStruct
    return pl.pallas_call(
        forward_kernel,
        grid=(head_count,),
        out_shape=(
            struct((head_count, total, DH), BF),
            struct((head_count, total, DH), BF),
            struct((head_count, total, DH), BF),
            struct((head_count, LONG, LONG), BF),
            struct((head_count, rest, rest), BF),
            struct((head_count, total, DH), BF),
            struct((4, size, width), BF),
        ),
        in_specs=[
            smem(),
            smem(),
            *(whole(size, width) for _ in range(4)),
            by_head(width, 3 * DH),
            by_head(QT, QT + 2 * NEAR),
            whole(rest, 1),
            whole(1, rest),
            whole(head_count * DH, width),
        ],
        out_specs=(
            by_head(total, DH),
            by_head(total, DH),
            by_head(total, DH),
            by_head(LONG, LONG),
            by_head(rest, rest),
            by_head(total, DH),
            whole(4, size, width),
        ),
        scratch_shapes=[pltpu.VMEM((total, head_count * DH), BF)],
        compiler_params=params(),
        cost_estimate=pl.CostEstimate(
            flops=10_000_000_000, bytes_accessed=20_000_000, transcendentals=4_000_000
        ),
        name="attend_forward",
    )(place, table, *blocks, weights, near, row_segment, key_segment, output_weight)


def backward_kernel(
    place_ref,
    grad0,
    grad1,
    grad2,
    grad3,
    block0,
    block1,
    block2,
    block3,
    weight_ref,
    output_weight_ref,
    query_ref,
    key_ref,
    value_ref,
    prob_ref,
    rest_ref,
    context_ref,
    normed_grad_ref,
    weight_grad_ref,
    output_grad_ref,
    line_ref,
    normed_total,
    context_grad,
    near_total,
    far_total,
    parts,
    key_total,
    value_total,
):
    head = pl.program_id(0)
    head_count = pl.num_programs(0)
    place = place_ref[0]
    size = block0.shape[0]
    total = query_ref.shape[1]
    spots = [pl.multiple_of((place ^ step) * size, size) for step in range(4)]
    output_grad = jnp.zeros(output_grad_ref.shape[1:], F32)
    for row, grad in zip(spots, (grad0, grad1, grad2, grad3)):
        context_grad[pl.ds(row, size), :] = dot(grad[...], output_weight_ref[0], ROWS_T).astype(BF)
        output_grad += dot(context_ref[0, pl.ds(row, size), :], grad[...], T_ROWS)
    output_grad_ref[0] = output_grad
    near_total[...] = jnp.zeros_like(near_total)
    far_total[...] = jnp.zeros_like(far_total)

    def tiles(first, keys, stored_ref):
        for tile in range(keys // QT):
            low, high, lane = pieces_of(tile, keys)
            rows = slice(first + tile * QT, first + tile * QT + QT)
            span = slice(first, first + keys)
            local = slice(tile * QT, tile * QT + QT)
            grads = context_grad[rows, :]
            prob = stored_ref[0, local, :]
            prob_grad = dot(grads, value_ref[0, span, :], ROWS_T)
            row_dot = jnp.sum(
                grads.astype(F32) * context_ref[0, rows, :].astype(F32), axis=1, keepdims=True
            )
            score_grad = prob.astype(F32) * (prob_grad - row_dot)
            low_grad = score_grad.astype(BF)
            near_total[:, lane : lane + high - low] += score_grad[:, low:high]
            for side, (a, b) in enumerate(((0, low), (high, keys))):
                if b > a:
                    far_total[side] += sum(
                        score_grad[:, c : c + 128] for c in range(a, b, 128)
                    )
            parts[rows, :DH] = dot(low_grad, key_ref[0, span, :]).astype(BF)
            value_part = dot(grads, prob, T_ROWS)
            key_part = dot(query_ref[0, rows, :], low_grad, T_ROWS)
            if tile == 0:
                value_total[:, span] = value_part
                key_total[:, span] = key_part
            else:
                value_total[:, span] += value_part
                key_total[:, span] += key_part

    tiles(0, LONG, prob_ref)
    if total > LONG:
        tiles(LONG, total - LONG, rest_ref)

    padded = jnp.concatenate(
        [near_total[...], jnp.zeros((QT, WIDE - near_total.shape[1]), F32)], axis=1
    )
    count = QT
    while count > 1:
        count //= 2
        padded = padded[:count] + pltpu.roll(padded[count:], WIDE - count, 1)
    line = pltpu.roll(padded, QT - 1, 1)
    lanes = lax.broadcasted_iota(jnp.int32, line.shape, 1)
    line = jnp.where(lanes == 0, jnp.sum(far_total[0]), line)
    line_ref[0] = jnp.where(lanes == WIDE - 1, jnp.sum(far_total[1]), line)

    key_low = key_total[...].astype(BF)
    value_low = value_total[...].astype(BF)
    parts[:, DH : 2 * DH] = key_total[...].T.astype(BF)
    parts[:, 2 * DH :] = value_total[...].T.astype(BF)
    weight_grad = jnp.zeros(weight_grad_ref.shape[1:], F32)
    for step, (row, block) in enumerate(zip(spots, (block0, block1, block2, block3))):
        taken = parts[pl.ds(row, size), :]
        made = dot(taken, weight_ref[0], ROWS_T)
        weight_grad += dot(taken, block[...], T_ROWS)

        @pl.when(head == 0)
        def _():
            normed_total[step] = made

        @pl.when(head > 0)
        def _():
            normed_total[step] += made

        @pl.when(head == head_count - 1)
        def _():
            normed_grad_ref[step] = normed_total[step].astype(BF)

    weight_grad_ref[0] = weight_grad


def attend_backward(place, grads, blocks, weights, output_weights, kept):
    head_count, width, _ = weights.shape
    size = blocks[0].shape[0]
    total = 4 * size
    rest = total - LONG
    by_head = lambda *shape: pl.BlockSpec((1, *shape), lambda h: (h, *(0 for _ in shape)))
    whole = lambda *shape: pl.BlockSpec(shape, lambda h: tuple(0 for _ in shape))
    struct = jax.ShapeDtypeStruct
    return pl.pallas_call(
        backward_kernel,
        grid=(head_count,),
        out_shape=(
            struct((4, size, width), BF),
            struct((head_count, 3 * DH, width), F32),
            struct((head_count, DH, width), F32),
            struct((head_count, 1, WIDE), F32),
        ),
        in_specs=[
            smem(),
            *(whole(size, width) for _ in range(8)),
            by_head(width, 3 * DH),
            by_head(DH, width),
            by_head(total, DH),
            by_head(total, DH),
            by_head(total, DH),
            by_head(LONG, LONG),
            by_head(rest, rest),
            by_head(total, DH),
        ],
        out_specs=(
            whole(4, size, width),
            by_head(3 * DH, width),
            by_head(DH, width),
            by_head(1, WIDE),
        ),
        scratch_shapes=[
            pltpu.VMEM((4, size, width), F32),
            pltpu.VMEM((total, DH), BF),
            pltpu.VMEM((QT, QT + 2 * NEAR), F32),
            pltpu.VMEM((2, QT, 128), F32),
            pltpu.VMEM((total, 3 * DH), BF),
            pltpu.VMEM((DH, total), F32),
            pltpu.VMEM((DH, total), F32),
        ],
        compiler_params=params(),
        cost_estimate=pl.CostEstimate(
            flops=20_000_000_000, bytes_accessed=20_000_000, transcendentals=0
        ),
        name="attend_backward",
    )(place, *grads, *blocks, weights, output_weights, *kept)


def across(values, axis, flip):
    count = lax.axis_size(axis)
    return lax.ppermute(values, axis, [(i, i ^ flip) for i in range(count)])


def gather_blocks(block):
    far = across(block, "tensor", 2)
    return (block, across(block, "tensor", 1), far, across(far, "tensor", 1))


def scatter_sum(parts):
    sibling = across(jnp.stack([parts[1], parts[3]]), "tensor", 1)
    outward = (parts[2].astype(F32) + sibling[1].astype(F32)).astype(BF)
    far = across(outward, "tensor", 2)
    return parts[0].astype(F32) + sibling[0].astype(F32) + far.astype(F32)


def sum_over_dp(values):
    count = lax.axis_size("dp")
    if count & (count - 1):
        return lax.psum(values, "dp")
    index = lax.axis_index("dp")
    bits = count.bit_length() - 1
    for bit in range(bits):
        half = values.shape[0] // 2
        mine = (index >> bit) & 1
        keep = lax.dynamic_slice_in_dim(values, mine * half, half)
        away = lax.dynamic_slice_in_dim(values, (1 - mine) * half, half)
        came = across(away.astype(BF), "dp", 1 << bit)
        values = keep + came.astype(F32)
    values = values.astype(BF)
    for bit in reversed(range(bits)):
        mine = (index >> bit) & 1
        came = across(values, "dp", 1 << bit)
        first = jnp.where(mine == 0, values, came)
        second = jnp.where(mine == 0, came, values)
        values = jnp.concatenate([first, second])
    return values.astype(F32)


def sum_small(values, axis):
    count = lax.axis_size(axis)
    if count & (count - 1) or count > 8:
        return lax.psum(values, axis)
    return values + sum(across(values, axis, flip) for flip in range(1, count))


def root_norm(values, gains):
    inverse = lax.rsqrt(jnp.mean(values * values, axis=-1, keepdims=True) + EPSILON)
    return (values * inverse * gains, inverse)


def norm_input_grad(values, inverse, gains, upstream):
    scaled = upstream * gains
    projection = jnp.mean(scaled * values, axis=-1, keepdims=True)
    return inverse * scaled - values * (inverse * inverse * inverse) * projection


def norm_gain_grad(values, inverse, upstream):
    return jnp.sum(upstream * values * inverse, axis=0)


def smooth_gate(values):
    return jax.nn.gelu(values, approximate=True)


def body(
    inputs,
    segments,
    first_gain,
    query_weight,
    lookup_projection,
    value_weight,
    output_weight,
    bucket_bias_table,
    second_gain,
    inner_weight,
    outer_weight,
    cotangent,
):
    total = segments.shape[0]
    width = inputs.shape[1]
    head_count = query_weight.shape[1] // DH
    gain_one = first_gain.astype(F32)
    gain_two = second_gain.astype(F32)
    factor = float(total * lax.axis_size("dp")) ** (-0.5)
    place = lax.axis_index("tensor").astype(jnp.int32).reshape(1)
    table = bucket_bias_table.astype(F32)
    heads = lambda weight: weight.reshape(width, head_count, DH).transpose(1, 0, 2)
    weights = jnp.concatenate(
        [heads(query_weight), heads(lookup_projection), heads(value_weight)], axis=2
    )
    near = near_bias(table)
    row_segment = segments[LONG:].reshape(-1, 1)
    key_segment = segments[LONG:].reshape(1, -1)

    norm_input = inputs.astype(F32)
    normed_value, inverse_one = root_norm(norm_input, gain_one)
    normed_one = gather_blocks(normed_value.astype(BF))
    *kept, attended = attend_forward(
        place, table, normed_one, weights, near, row_segment, key_segment, output_weight
    )
    cotangents = gather_blocks(cotangent)
    middle = norm_input + scatter_sum(attended)
    normed_value, inverse_two = root_norm(middle, gain_two)
    normed_two = jnp.concatenate(gather_blocks(normed_value.astype(BF)))
    full_cotangent = jnp.concatenate(cotangents)
    inner_value = dot(normed_two, inner_weight)
    hidden_value, gate_pullback = jax.vjp(smooth_gate, inner_value)
    hidden = hidden_value.astype(BF)
    outer_part = dot(hidden, outer_weight).astype(BF).reshape(4, -1, width)
    hidden_grad = dot(full_cotangent, outer_weight, ROWS_T)
    inner_grad = gate_pullback(hidden_grad)[0].astype(BF)
    second_part = dot(inner_grad, inner_weight, ROWS_T).astype(BF).reshape(4, -1, width)
    outer_weight_grad = dot(hidden, full_cotangent, T_ROWS)
    inner_weight_grad = dot(normed_two, inner_grad, T_ROWS)
    normed_two_grad = scatter_sum(second_part)
    layer_output = (middle + scatter_sum(outer_part)).astype(BF)
    middle_grad = cotangent.astype(F32) + norm_input_grad(
        middle, inverse_two, gain_two, normed_two_grad
    )
    gain_two_part = norm_gain_grad(middle, inverse_two, normed_two_grad)
    attended_grad = gather_blocks(middle_grad.astype(BF))
    normed_one_part, weight_grads, output_weight_grad, line = attend_backward(
        place,
        attended_grad,
        normed_one,
        weights,
        output_weight.reshape(head_count, DH, width),
        kept,
    )
    normed_one_grad = scatter_sum(normed_one_part)
    input_grad = middle_grad + norm_input_grad(norm_input, inverse_one, gain_one, normed_one_grad)
    gain_one_part = norm_gain_grad(norm_input, inverse_one, normed_one_grad)
    gain_grads = jnp.stack([gain_one_part, gain_two_part])
    gain_grads = sum_small(sum_small(gain_grads, "tensor"), "dp")

    slots = jnp.arange(table.shape[0], dtype=jnp.int32)
    offsets = jnp.arange(WIDE, dtype=jnp.int32) - (QT + NEAR - 1)
    chosen = buckets_of(offsets)[None, :] == slots[:, None]
    table_grad = jnp.sum(
        jnp.where(chosen[:, None, :], line.reshape(1, head_count, WIDE), 0.0), axis=2
    )
    table_grad = sum_small(table_grad, "dp")
    outer_weight_grad = sum_over_dp(outer_weight_grad)
    inner_weight_grad = sum_over_dp(inner_weight_grad)
    rows = head_count * DH
    small = jnp.concatenate(
        [weight_grads.reshape(3 * rows, width), output_weight_grad.reshape(rows, width)]
    )
    small = sum_over_dp(small)
    three = small[: 3 * rows].reshape(head_count, 3, DH, width).transpose(1, 3, 0, 2)
    three = three.reshape(3, width, rows)
    return (
        layer_output,
        input_grad,
        three[0] * factor,
        three[1] * factor,
        three[2] * factor,
        small[3 * rows :] * factor,
        table_grad * factor,
        inner_weight_grad * factor,
        outer_weight_grad * factor,
        gain_grads * factor,
    )


def solution(mesh):
    return jax.shard_map(
        body,
        mesh=mesh,
        in_specs=(
            P(("dp", "tensor"), None),
            P("dp"),
            P(),
            P(None, "tensor"),
            P(None, "tensor"),
            P(None, "tensor"),
            P("tensor", None),
            P(None, "tensor"),
            P(),
            P(None, "tensor"),
            P("tensor", None),
            P(("dp", "tensor"), None),
        ),
        out_specs=(
            P(("dp", "tensor"), None),
            P(("dp", "tensor"), None),
            P(None, "tensor"),
            P(None, "tensor"),
            P(None, "tensor"),
            P("tensor", None),
            P(None, "tensor"),
            P(None, "tensor"),
            P("tensor", None),
            P(),
        ),
        check_vma=False,
    )
```

```python
import functools

import jax
import jax.numpy as jnp
from jax import lax
from jax.experimental import pallas as pl
from jax.experimental.pallas import tpu as pltpu
from jax.sharding import PartitionSpec as P

DH = 64
LONG = 1024
QT = 256
NEAR = 128
WIDE = 768
RIDER = 16
EDGES = (8, 12, 16, 23, 32, 46, 64, 91)
EPSILON = 1e-06
MASKED = -1000000000.0
BF = jnp.bfloat16
F32 = jnp.float32


def buckets_of(offset):
    distance = jnp.abs(offset)
    coarse = jnp.full(distance.shape, 7, jnp.int32)
    for boundary in EDGES:
        coarse = coarse + (distance >= boundary).astype(jnp.int32)
    bucket = jnp.where(distance < 8, distance, coarse)
    return bucket + jnp.where(offset > 0, 16, 0).astype(jnp.int32)


def dot(left, right, dims=((1,), (0,))):
    return lax.dot_general(left, right, (dims, ((), ())), preferred_element_type=F32)


ROWS_T = ((1,), (1,))
T_ROWS = ((0,), (0,))


FREE = pl.CostEstimate(flops=0, bytes_accessed=0, transcendentals=0)
LONG_KERNEL = pl.CostEstimate(flops=200_000_000_000, bytes_accessed=0, transcendentals=0)


def params(limit=30):
    return pltpu.CompilerParams(vmem_limit_bytes=limit * 1024 * 1024)


def struct(shape, dtype):
    return jax.ShapeDtypeStruct(shape, dtype)


def one(shape, *index):
    index = index + (0,) * (len(shape) - len(index))
    return pl.BlockSpec(shape, lambda i: index)


def call(kernel, name, outs, ins, operands, scratch=(), cost=FREE):
    spec = lambda item: item if isinstance(item, pl.BlockSpec) else one(item.shape)
    return pl.pallas_call(
        kernel,
        grid=(1,),
        out_shape=outs,
        in_specs=[spec(item) for item in ins],
        out_specs=tuple(one(o.shape) for o in outs),
        scratch_shapes=scratch,
        compiler_params=params(),
        cost_estimate=cost,
        name=name,
    )(*operands)


def vmem():
    return pl.BlockSpec(memory_space=pltpu.VMEM)


def smem():
    return pl.BlockSpec(memory_space=pltpu.SMEM)


def near_kernel(table_ref, near_ref):
    head_count = near_ref.shape[0]
    lane = lax.broadcasted_iota(jnp.int32, (8, WIDE), 1)
    bucket = buckets_of(lane - (QT + NEAR - 1))
    for head in range(head_count):
        line = jnp.zeros((8, WIDE), F32)
        for slot in range(table_ref.shape[0]):
            line = jnp.where(bucket == slot, table_ref[slot, head], line)
        rows = jnp.broadcast_to(line[:1], (QT, WIDE))
        turned = pltpu.roll(rows, WIDE - QT + 1, 1, stride=1, stride_axis=0)
        near_ref[head] = turned[:, : QT + 2 * NEAR]


def near_bias(table):
    head_count = table.shape[1]
    return pl.pallas_call(
        near_kernel,
        out_shape=jax.ShapeDtypeStruct((head_count, QT, QT + 2 * NEAR), F32),
        in_specs=[smem()],
        out_specs=vmem(),
        compiler_params=params(),
        name="near_bias",
    )(table)


def pieces_of(tile, keys):
    low = max(tile * QT - NEAR, 0)
    high = min(tile * QT + QT + NEAR, keys)
    return low, high, low - (tile * QT - NEAR)


def tiles_of(total):
    ranges = [(0, LONG)] + ([(LONG, total - LONG)] if total > LONG else [])
    return [
        (first + tile * QT, first, keys, tile)
        for first, keys in ranges
        for tile in range(keys // QT)
    ]


def stored_tile(spots, head, tile, prob, rest):
    row, first, keys, number = spots[tile]
    return (rest if first else prob).at[head, pl.ds(number * QT, QT), :]


def forward_kernel(
    place_ref,
    table_ref,
    block0,
    block1,
    block2,
    block3,
    gain_ref,
    query_weight_ref,
    key_weight_ref,
    value_weight_ref,
    near_ref,
    row_segment_ref,
    key_segment_ref,
    output_weight_ref,
    packed_ref,
    prob_out,
    rest_out,
    normed_out,
    send_ref,
    keep_ref,
    gathered,
    query,
    key,
    value,
    normed,
    prob,
    rest,
    weight,
    sems,
    normed_sem,
):
    head = pl.program_id(0)
    head_count = pl.num_programs(0)
    place = place_ref[0]
    for which, ref in enumerate((query_weight_ref, key_weight_ref, value_weight_ref)):
        weight[which * DH : which * DH + DH, :] = ref[...]
    blocks = (block0, block1, block2, block3)
    size = block0.shape[0]
    normed_copy = pltpu.make_async_copy(normed, normed_out, normed_sem)

    @pl.when(head == 0)
    def _():
        for step, block in enumerate(blocks):
            values = block[...].astype(F32)
            inverse = inverse_root(values)
            normed[step] = (values * inverse * gain_ref[...].astype(F32)).astype(BF)
        normed_copy.start()

    for step in range(4):
        row = pl.multiple_of((place ^ step) * size, size)
        rows = pl.ds(row, size)
        made = dot(normed[step], weight[...], ROWS_T).astype(BF)
        packed_ref[0, rows, : 3 * DH] = made
        query[rows, :] = made[:, :DH]
        key[rows, :] = made[:, DH : 2 * DH]
        value[rows, :] = made[:, 2 * DH :]
    total = query.shape[0]
    left_bias = table_ref[15, head]
    right_bias = table_ref[31, head]
    spots = tiles_of(total)

    def copy_of(which, tile):
        return pltpu.make_async_copy(
            stored_tile(spots, which, tile, prob, rest),
            stored_tile(spots, which, tile, prob_out, rest_out),
            sems.at[which, tile],
        )

    for index, (row, first, keys, tile) in enumerate(spots):
        low, high, lane = pieces_of(tile, keys)
        rows = slice(row, row + QT)
        local = slice(tile * QT, tile * QT + QT)
        store = rest if first else prob
        scores = dot(query[rows, :], key[first : first + keys, :], ROWS_T)
        parts = []
        if low > 0:
            parts.append((0, low, scores[:, :low] + left_bias))
        parts.append((low, high, scores[:, low:high] + near_ref[0, :, lane : lane + high - low]))
        if high < keys:
            parts.append((high, keys, scores[:, high:] + right_bias))
        if first:
            row_segment = row_segment_ref[local, :]
            parts = [
                (a, b, jnp.where(row_segment == key_segment_ref[:, a:b], part, MASKED))
                for a, b, part in parts
            ]
        peak = functools.reduce(
            jnp.maximum, [jnp.max(part, axis=1, keepdims=True) for a, b, part in parts]
        )
        parts = [(a, b, jnp.exp(part - peak)) for a, b, part in parts]
        whole = sum(jnp.sum(part, axis=1, keepdims=True) for a, b, part in parts)
        share = 1.0 / whole
        for a, b, part in parts:
            store[head, local, a:b] = (part * share).astype(BF)
        made = dot(store[head, local, :], value[first : first + keys, :]).astype(BF)
        packed_ref[0, rows, 3 * DH :] = made
        copy_of(head, index).start()
    for which in range(gathered.shape[1] // DH):

        @pl.when(head == which)
        def _():
            gathered[:, which * DH : which * DH + DH] = packed_ref[0, :, 3 * DH :]

    @pl.when(head == head_count - 1)
    def _():
        for step in (1, 3, 2, 0):
            row = pl.multiple_of((place ^ step) * size, size)
            made = dot(gathered[pl.ds(row, size), :], output_weight_ref[...]).astype(BF)
            out = send_ref if step & 1 else keep_ref
            out[step >> 1] = made
        normed_copy.wait()
        for which in range(gathered.shape[1] // DH):
            for index in range(len(spots)):
                copy_of(which, index).wait()


def attend_forward(place, table, blocks, gain, weights, near, row_segment, key_segment, output_weight):
    size, width = blocks[0].shape
    head_count = near.shape[0]
    total = 4 * size
    rest = total - LONG
    by_head = lambda *shape: pl.BlockSpec((1, *shape), lambda h: (h, *(0 for _ in shape)))
    whole = lambda *shape: pl.BlockSpec(shape, lambda h: tuple(0 for _ in shape))
    apart = pl.BlockSpec(memory_space=pl.ANY)
    return pl.pallas_call(
        forward_kernel,
        grid=(head_count,),
        out_shape=(
            struct((head_count, total, 4 * DH), BF),
            struct((head_count, LONG, LONG), BF),
            struct((head_count, rest, rest), BF),
            struct((4, size, width), BF),
            struct((2, size, width), BF),
            struct((2, size, width), BF),
            struct((total, head_count * DH), BF),
        ),
        in_specs=[
            smem(),
            smem(),
            *(whole(size, width) for _ in range(4)),
            whole(1, width),
            *(pl.BlockSpec((DH, width), lambda h: (h, 0)) for _ in range(3)),
            by_head(QT, QT + 2 * NEAR),
            whole(rest, 1),
            whole(1, rest),
            whole(head_count * DH, width),
        ],
        out_specs=(
            by_head(total, 4 * DH),
            apart,
            apart,
            apart,
            whole(2, size, width),
            whole(2, size, width),
            whole(total, head_count * DH),
        ),
        scratch_shapes=[
            pltpu.VMEM((total, DH), BF),
            pltpu.VMEM((total, DH), BF),
            pltpu.VMEM((total, DH), BF),
            pltpu.VMEM((4, size, width), BF),
            pltpu.VMEM((head_count, LONG, LONG), BF),
            pltpu.VMEM((head_count, rest, rest), BF),
            pltpu.VMEM((3 * DH, width), BF),
            pltpu.SemaphoreType.DMA((head_count, total // QT)),
            pltpu.SemaphoreType.DMA,
        ],
        compiler_params=params(56),
        cost_estimate=LONG_KERNEL,
        name="attend_forward",
    )(place, table, *blocks, gain, *weights, near, row_segment, key_segment, output_weight)


def backward_kernel(
    place_ref,
    grad0,
    grad1,
    grad2,
    grad3,
    normed_in,
    output_weight_ref,
    packed_ref,
    gathered_ref,
    prob_in,
    rest_in,
    parts_ref,
    line_ref,
    kept_ref,
    away_ref,
    *more_refs,
):
    (
        normed,
        prob,
        rest,
        query,
        key,
        value,
        context,
        turned,
        context_grad,
        near_total,
        far_total,
        key_total,
        value_total,
        sums,
        sems,
        normed_sem,
    ) = more_refs
    head = pl.program_id(0)
    head_count = pl.num_programs(0)
    place = place_ref[0]
    bit = place_ref[1] & 1
    size = normed.shape[1]
    total = query.shape[0]
    spots = tiles_of(total)
    blocks = [pl.multiple_of((place ^ step) * size, size) for step in range(4)]
    normed_copy = pltpu.make_async_copy(normed_in, normed, normed_sem)

    def copy_of(which, tile):
        return pltpu.make_async_copy(
            stored_tile(spots, which, tile, prob_in, rest_in),
            stored_tile(spots, which, tile, prob, rest),
            sems.at[which, tile],
        )

    @pl.when(head == 0)
    def _():
        for which in range(prob.shape[0]):
            for index in range(len(spots)):
                copy_of(which, index).start()
            if which == 0:
                normed_copy.start()

    query[...] = packed_ref[0, :, :DH]
    key[...] = packed_ref[0, :, DH : 2 * DH]
    value[...] = packed_ref[0, :, 2 * DH : 3 * DH]
    context[...] = packed_ref[0, :, 3 * DH :]
    turned[...] = key[...].T
    whole = sums.shape[0] // 4

    @pl.when(head == 0)
    def _():
        output_grad = 0.0
        for row, grad in zip(blocks, (grad0, grad1, grad2, grad3)):
            rows = pl.ds(row, size)
            made = dot(grad[...], output_weight_ref[...], ROWS_T).astype(BF)
            for which in range(context_grad.shape[0]):
                context_grad[which, rows, :] = made[:, which * DH : which * DH + DH]
            output_grad += dot(gathered_ref[rows, :], grad[...], T_ROWS)
        sums[3 * whole :, :] = output_grad

    near_total[...] = jnp.zeros_like(near_total)
    far_total[...] = jnp.zeros_like(far_total)

    for index, (row, first, keys, tile) in enumerate(spots):
        low, high, lane = pieces_of(tile, keys)
        rows = slice(row, row + QT)
        span = slice(first, first + keys)
        local = slice(tile * QT, tile * QT + QT)
        grads = context_grad[head, rows, :]
        prob_grad = dot(grads, value[span, :], ROWS_T)
        row_dot = jnp.sum(
            grads.astype(F32) * context[rows, :].astype(F32), axis=1, keepdims=True
        )
        copy_of(head, index).wait()
        taken = (rest if first else prob)[head, local, :]
        score_grad = taken.astype(F32) * (prob_grad - row_dot)
        low_grad = score_grad.astype(BF)
        near_total[:, lane : lane + high - low] += score_grad[:, low:high]
        for side, (a, b) in enumerate(((0, low), (high, keys))):
            if b > a:
                far_total[side] += sum(score_grad[:, c : c + 128] for c in range(a, b, 128))
        parts_ref[0, :DH, rows] = dot(turned[:, span], low_grad, ROWS_T).astype(BF)
        value_part = dot(grads, taken, T_ROWS)
        key_part = dot(query[rows, :], low_grad, T_ROWS)
        if tile == 0:
            value_total[:, span] = value_part
            key_total[:, span] = key_part
        else:
            value_total[:, span] += value_part
            key_total[:, span] += key_part

    padded = jnp.concatenate(
        [near_total[...], jnp.zeros((QT, WIDE - near_total.shape[1]), F32)], axis=1
    )
    count = QT
    while count > 1:
        count //= 2
        padded = padded[:count] + pltpu.roll(padded[count:], WIDE - count, 1)
    line = pltpu.roll(padded, QT - 1, 1)
    lanes = lax.broadcasted_iota(jnp.int32, line.shape, 1)
    line = jnp.where(lanes == 0, jnp.sum(far_total[0]), line)
    line_ref[0] = jnp.where(lanes == WIDE - 1, jnp.sum(far_total[1]), line)

    parts_ref[0, DH : 2 * DH, :] = key_total[...].astype(BF)
    parts_ref[0, 2 * DH :, :] = value_total[...].astype(BF)

    @pl.when(head == 0)
    def _():
        normed_copy.wait()

    made = sum(
        dot(parts_ref[0, :, pl.ds(row, size)], normed[step])
        for step, row in enumerate(blocks)
    )
    for which in range(3):
        row = pl.multiple_of(which * whole + head * DH, DH)
        sums[pl.ds(row, DH), :] = made[which * DH : which * DH + DH]

    @pl.when(head == head_count - 1)
    def _():
        half = kept_ref.shape[0]
        for flip, out in enumerate((kept_ref, away_ref)):
            row = pl.multiple_of((bit ^ flip) * half, half)
            out[...] = sums[pl.ds(row, half), :].astype(out.dtype)


def attend_backward(place, grads, normed, output_weights, kept):
    packed, prob, rest, gathered = kept
    _, size, width = normed.shape
    head_count, total, _ = packed.shape
    rows = 4 * DH * head_count
    by_head = lambda *shape: pl.BlockSpec((1, *shape), lambda h: (h, *(0 for _ in shape)))
    whole = lambda *shape: pl.BlockSpec(shape, lambda h: tuple(0 for _ in shape))
    apart = pl.BlockSpec(memory_space=pl.ANY)
    return pl.pallas_call(
        backward_kernel,
        grid=(head_count,),
        out_shape=(
            struct((head_count, 3 * DH, total), BF),
            struct((head_count, 1, WIDE), F32),
            struct((rows // 2, width), F32),
            struct((rows // 2, width), BF),
        ),
        in_specs=[
            smem(),
            *(whole(size, width) for _ in range(4)),
            apart,
            whole(head_count * DH, width),
            by_head(total, 4 * DH),
            whole(total, head_count * DH),
            apart,
            apart,
        ],
        out_specs=(
            by_head(3 * DH, total),
            by_head(1, WIDE),
            whole(rows // 2, width),
            whole(rows // 2, width),
        ),
        scratch_shapes=[
            pltpu.VMEM(normed.shape, BF),
            pltpu.VMEM(prob.shape, BF),
            pltpu.VMEM(rest.shape, BF),
            *(pltpu.VMEM((total, DH), BF) for _ in range(4)),
            pltpu.VMEM((DH, total), BF),
            pltpu.VMEM((head_count, total, DH), BF),
            pltpu.VMEM((QT, QT + 2 * NEAR), F32),
            pltpu.VMEM((2, QT, 128), F32),
            pltpu.VMEM((DH, total), F32),
            pltpu.VMEM((DH, total), F32),
            pltpu.VMEM((rows, width), F32),
            pltpu.SemaphoreType.DMA((head_count, total // QT)),
            pltpu.SemaphoreType.DMA,
        ],
        compiler_params=params(40),
        cost_estimate=LONG_KERNEL,
        name="attend_backward",
    )(place, *grads, normed, output_weights, packed, gathered, prob, rest)


def normed_grad_kernel(
    place_ref,
    parts_ref,
    query_weight_ref,
    key_weight_ref,
    value_weight_ref,
    gain_ref,
    normed_ref,
    gain_two_ref,
    line_ref,
    away_ref,
    send_ref,
    keep_ref,
    rider_ref,
    loaded_ref,
):
    place = place_ref[0]
    size = normed_ref.shape[1]
    gain_grad = 0.0
    weights = (query_weight_ref, key_weight_ref, value_weight_ref)
    for step in range(4):
        row = pl.multiple_of((place ^ step) * size, size)
        made = 0.0
        for head in range(parts_ref.shape[0]):
            weight = jnp.concatenate([ref[head * DH : head * DH + DH, :] for ref in weights])
            made += dot(parts_ref[head, :, pl.ds(row, size)], weight, T_ROWS)
        out = send_ref if step & 1 else keep_ref
        out[step >> 1] = made.astype(BF)
        gain_grad += jnp.sum(made * normed_ref[step].astype(F32), axis=0, keepdims=True)
    rider_ref[...] = jnp.zeros_like(rider_ref)
    rider_ref[0:1, :] = gain_grad / gain_ref[...].astype(F32)
    rider_ref[1:2, :] = gain_two_ref[...]
    for head in range(line_ref.shape[0]):
        rider_ref[2 + head : 3 + head, :] = line_ref[head]
    half = away_ref.shape[0]
    loaded_ref[:half, :] = away_ref[...]
    loaded_ref[half:, :] = rider_ref[...].astype(BF)


def normed_grad(place, parts, weights, gain, normed, gain_two_grad, lines, away):
    _, size, width = normed.shape
    operands = (parts, *weights, gain, normed, gain_two_grad, lines, away)
    return call(
        normed_grad_kernel,
        "normed_grad",
        (
            struct((2, size, width), BF),
            struct((2, size, width), BF),
            struct((RIDER, width), F32),
            struct((away.shape[0] + RIDER, width), BF),
        ),
        (smem(), *operands),
        (place, *operands),
        cost=LONG_KERNEL,
    )


def inverse_root(values):
    return lax.rsqrt(jnp.mean(values * values, axis=-1, keepdims=True) + EPSILON)


def norm_input_grad(values, inverse, gains, upstream):
    scaled = upstream * gains
    projection = jnp.mean(scaled * values, axis=-1, keepdims=True)
    return inverse * scaled - values * (inverse * inverse * inverse) * projection


def middle_grad_kernel(
    cotangent_ref, middle_ref, own_ref, near_ref, far_ref, gain_ref, grad_ref, low_ref, gain_grad_ref
):
    upstream = own_ref[...].astype(F32) + near_ref[...].astype(F32) + far_ref[...].astype(F32)
    values = middle_ref[...]
    inverse = inverse_root(values)
    grad = cotangent_ref[...].astype(F32) + norm_input_grad(
        values, inverse, gain_ref[...].astype(F32), upstream
    )
    grad_ref[...] = grad
    low_ref[...] = grad.astype(BF)
    gain_grad_ref[...] = jnp.sum(upstream * values * inverse, axis=0, keepdims=True)


def make_middle_grad(cotangent, middle, sums, gain):
    shape = middle.shape
    operands = (cotangent, middle, *sums, gain)
    return call(
        middle_grad_kernel,
        "middle_grad",
        (struct(shape, F32), struct(shape, BF), struct((1, shape[1]), F32)),
        operands,
        operands,
    )


def input_grad_kernel(input_ref, own_ref, near_ref, far_ref, gain_ref, middle_ref, out_ref):
    upstream = own_ref[0].astype(F32) + near_ref[0].astype(F32) + far_ref[...].astype(F32)
    values = input_ref[...].astype(F32)
    out_ref[...] = middle_ref[...] + norm_input_grad(
        values, inverse_root(values), gain_ref[...], upstream
    )


def make_input_grad(inputs, sums, gain, middle_grad):
    first = one((1, *inputs.shape))
    return call(
        input_grad_kernel,
        "input_grad",
        (struct(inputs.shape, F32),),
        (inputs, first, first, sums[2], gain, middle_grad),
        (inputs, *sums, gain, middle_grad),
    )[0]


def layer_output_kernel(middle_ref, own_ref, near_ref, far_ref, out_ref):
    own, near, far = (ref[...].astype(F32) for ref in (own_ref, near_ref, far_ref))
    out_ref[...] = (middle_ref[...] + (own + near + far)).astype(BF)


def make_layer_output(middle, sums):
    operands = (middle, *sums)
    return call(
        layer_output_kernel, "layer_output", (struct(middle.shape, BF),), operands, operands
    )[0]


def outer_kernel(weight_ref, *refs):
    hidden_refs, out_refs = refs[:4], refs[4:]
    for hidden, out in zip(hidden_refs, out_refs):
        out[...] = dot(hidden[...], weight_ref[...]).astype(BF)


def outer_product(hidden, weight):
    operands = (weight, *hidden)
    shape = struct((hidden[0].shape[0], weight.shape[1]), BF)
    return call(outer_kernel, "outer", (shape,) * 4, operands, operands, cost=LONG_KERNEL)


def after(values, *others):
    return lax.optimization_barrier((values, others))[0]


def across(values, axis, flip):
    count = lax.axis_size(axis)
    return lax.ppermute(values, axis, [(i, i ^ flip) for i in range(count)])


def over_core(values):
    return across(values, "tensor", 1)


def over_x(values):
    return across(values, "tensor", 2)


def usual():
    return lax.axis_size("dp") == 8


def split_kernel(place_ref, *refs):
    kept_ref, came_ref, *refs = refs
    riders, refs = refs[:-4], refs[-4:]
    own_ref, *away_refs = refs
    size = own_ref.shape[0]
    spot = place_ref[1] >> 1
    if riders:
        rider_ref, total_ref = riders
        half = kept_ref.shape[0]
        total_ref[...] = rider_ref[...] + came_ref[half:, :].astype(F32)
        for out in away_refs:
            out[size:, :] = total_ref[...].astype(BF)
    for flip, out in enumerate((own_ref, *away_refs)):
        rows = pl.ds(pl.multiple_of((spot ^ flip) * size, size), size)
        out[:size, :] = (kept_ref[rows, :] + came_ref[rows, :].astype(F32)).astype(out.dtype)


def four_kernel(own_ref, came0, came1, came2, *refs):
    *riders, out_ref = refs
    size = own_ref.shape[0]
    total = own_ref[...]
    for came in (came0, came1, came2):
        total += came[:size, :].astype(F32)
    out_ref[...] = total.astype(BF)
    if riders:
        rider_ref, sum_ref = riders
        total = rider_ref[...]
        for came in (came0, came1, came2):
            total += came[size:, :].astype(F32)
        sum_ref[...] = total


def join_kernel(place_ref, own_ref, came0, came1, came2, out_ref):
    size = own_ref.shape[0]
    spot = place_ref[1] >> 1
    for flip, ref in enumerate((own_ref, came0, came1, came2)):
        out_ref[pl.ds(pl.multiple_of((spot ^ flip) * size, size), size), :] = ref[...]


def whole_kernel(factor, pieces, place_ref, own_ref, came_ref, *refs):
    *out_refs, whole = refs
    part = own_ref.shape[0] // pieces
    bit = place_ref[1] & 1
    for flip, ref in enumerate((own_ref, came_ref)):
        for piece in range(pieces):
            row = pl.multiple_of((2 * piece + (bit ^ flip)) * part, part)
            whole[pl.ds(row, part), :] = ref[piece * part : piece * part + part, :]
    rows = whole.shape[0] // len(out_refs)
    for index, out in enumerate(out_refs):
        out[...] = whole[index * rows : index * rows + rows, :].astype(F32) * factor


def cut_kernel(place_ref, *refs):
    whole_refs, kept_ref, away_ref = refs[:-2], refs[-2], refs[-1]
    bit = place_ref[1] & 1
    half = whole_refs[0].shape[0] // 2
    for index, ref in enumerate(whole_refs):
        here = slice(index * half, index * half + half)
        for flip, out in enumerate((kept_ref, away_ref)):
            rows = pl.ds(pl.multiple_of((bit ^ flip) * half, half), half)
            out[here, :] = ref[rows, :].astype(out.dtype)


def cut(place, arrays):
    rows, width = arrays[0].shape
    shape = (len(arrays) * rows // 2, width)
    return call(
        cut_kernel, "cut", (struct(shape, F32), struct(shape, BF)), (smem(), *arrays), (place, *arrays)
    )


class Reduction:
    def __init__(self, name, place, pieces, kept, away, rider=None):
        self.name, self.place, self.pieces, self.rider = name, place, pieces, rider
        self.rows, self.width = 2 * kept.shape[0], kept.shape[1]
        self.stage = 0
        self.count = lax.axis_size("dp")
        self.halves = (kept, away[: kept.shape[0]])
        self.kept = kept
        if self.count == 8:
            self.came = across(away, "dp", 1)

    def step(self, *others):
        self.stage += 1
        if self.count != 8:
            if self.stage == 1 and self.rider is not None:
                self.rider = lax.psum(self.rider, "dp")
            return self.kept
        width = self.width
        name = f"{self.name}_{self.stage}"
        riders = () if self.rider is None else (self.rider,)
        also = tuple(struct(item.shape, F32) for item in riders)
        if self.stage == 1:
            size = self.rows // 8
            far = size + sum(item.shape[0] for item in riders)
            operands = (self.kept, after(self.came, *others), *riders)
            *riders, own, a, b, c = call(
                split_kernel,
                name,
                (*also, struct((size, width), F32), *(struct((far, width), BF) for _ in range(3))),
                (smem(), *operands),
                (self.place, *operands),
            )
            self.kept = own
            self.came = [across(item, "dp", 2 * flip) for flip, item in enumerate((a, b, c), 1)]
            self.rider = riders[0] if riders else None
            return own
        if self.stage == 2:
            operands = (self.kept, *after(self.came, *others), *riders)
            *riders, low = call(
                four_kernel, name, (*also, struct(self.kept.shape, BF)), operands, operands
            )
            self.kept = low
            self.came = [across(low, "dp", 2 * flip) for flip in range(1, 4)]
            self.rider = riders[0] if riders else None
            return low
        if self.stage == 3:
            operands = (self.kept, *after(self.came, *others))
            half = call(
                join_kernel,
                name,
                (struct((self.rows // 2, width), BF),),
                (smem(), *operands),
                (self.place, *operands),
            )[0]
            self.kept = half
            self.came = across(half, "dp", 1)
            return half
        raise ValueError("over")

    def finish(self, factor, count, *others):
        own, came = self.kept, self.came if self.count == 8 else None
        if self.count != 8:
            kept, away = self.halves
            bit = lax.axis_index("dp") & 1
            away = away.astype(F32)
            first = jnp.where(bit == 0, kept, away)
            second = jnp.where(bit == 0, away, kept)
            total = sum_over_dp(jnp.concatenate([first, second])).astype(BF)
            half = kept.shape[0]
            own = lax.dynamic_slice_in_dim(total, bit * half, half)
            came = lax.dynamic_slice_in_dim(total, (1 - bit) * half, half)
        operands = (own, after(came, *others))
        width = self.width
        return call(
            functools.partial(whole_kernel, factor, self.pieces),
            self.name,
            (struct((self.rows // count, width), F32),) * count,
            (smem(), *operands),
            (self.place, *operands),
            (pltpu.VMEM((self.rows, width), BF),),
        )


def sum_over_dp(values):
    count = lax.axis_size("dp")
    if count & (count - 1) or values.shape[0] % count:
        return lax.psum(values, "dp")
    index = lax.axis_index("dp")
    bits = count.bit_length() - 1
    for bit in range(bits):
        half = values.shape[0] // 2
        mine = (index >> bit) & 1
        keep = lax.dynamic_slice_in_dim(values, mine * half, half)
        away = lax.dynamic_slice_in_dim(values, (1 - mine) * half, half)
        values = keep + across(away.astype(BF), "dp", 1 << bit).astype(F32)
    values = values.astype(BF)
    for bit in reversed(range(bits)):
        mine = (index >> bit) & 1
        came = across(values, "dp", 1 << bit)
        first = jnp.where(mine == 0, values, came)
        second = jnp.where(mine == 0, came, values)
        values = jnp.concatenate([first, second])
    return values.astype(F32)


ROOT = 0.7978845608028654
CUBE = 0.044715


def gate(value):
    square = value * value
    tanh = jnp.tanh(ROOT * value * (1.0 + CUBE * square))
    half = 0.5 * (1.0 + tanh)
    slope = half + 0.5 * ROOT * value * (1.0 - tanh * tanh) * (1.0 + 3.0 * CUBE * square)
    return value * half, slope


def body(
    inputs,
    segments,
    first_gain,
    query_weight,
    lookup_projection,
    value_weight,
    output_weight,
    bucket_bias_table,
    second_gain,
    inner_weight,
    outer_weight,
    cotangent,
):
    total = segments.shape[0]
    size, width = inputs.shape
    head_count = query_weight.shape[1] // DH
    factor = float(total * lax.axis_size("dp")) ** (-0.5)

    far, near_block = over_x(inputs), over_core(inputs)
    place = jnp.stack([lax.axis_index("tensor"), lax.axis_index("dp")]).astype(jnp.int32)
    gain_one = first_gain.astype(F32)
    gain_two = second_gain.astype(F32)
    gain_row = gain_one.reshape(1, -1)
    table = bucket_bias_table.astype(F32)
    weights = (query_weight.T, lookup_projection.T, value_weight.T)
    near = near_bias(table)
    row_segment = segments[LONG:].reshape(-1, 1)
    key_segment = segments[LONG:].reshape(1, -1)
    norm_input = inputs.astype(F32)
    inverse_one = inverse_root(norm_input)
    far = after(far, near, row_segment, place, gain_row, inverse_one)
    blocks = (inputs, near_block, far, over_core(far))
    cot_far = over_x(after(cotangent, far))
    cot_near = over_core(after(cotangent, far))

    *kept, normed_one, send, keep, gathered = attend_forward(
        place, table, blocks, gain_row, weights, near, row_segment, key_segment, output_weight
    )
    kept.append(gathered)
    cot_far = after(cot_far, keep)
    near_sums = over_core(after(send, cot_far))
    outward = (keep[1].astype(F32) + near_sums[1].astype(F32)).astype(BF)
    far_sum = over_x(outward)
    cot_far = after(cot_far, outward)
    cotangents = (cotangent, cot_near, cot_far, over_core(cot_far))
    hidden_grads = {}
    for step in (2, 3):
        hidden_grads[step] = dot(cotangents[step], outer_weight, ROWS_T)
    far_sum = after(far_sum, hidden_grads)

    middle = norm_input + (
        keep[0].astype(F32) + near_sums[0].astype(F32) + far_sum.astype(F32)
    )
    inverse_two = inverse_root(middle)
    low = (middle * inverse_two * gain_two).astype(BF)
    normed_two = [low, over_core(low), over_x(low)]

    hidden, inner_grads, second = {}, {}, {}

    def feed(step):
        values, slope = gate(dot(normed_two[step], inner_weight))
        hidden[step] = values.astype(BF)
        if step not in hidden_grads:
            hidden_grads[step] = dot(cotangents[step], outer_weight, ROWS_T)
        inner_grads[step] = (hidden_grads[step] * slope).astype(BF)
        second[step] = dot(inner_grads[step], inner_weight, ROWS_T).astype(BF)

    def weight_grads(steps):
        outer = sum(dot(hidden[step], cotangents[step], T_ROWS) for step in steps)
        inner = sum(dot(normed_two[step], inner_grads[step], T_ROWS) for step in steps)
        return outer, inner

    feed(0)
    feed(1)
    second_near_one = over_core(second[1])
    first_grads = weight_grads((0, 1))
    normed_two[2] = after(normed_two[2], second, first_grads)
    normed_two.append(over_core(normed_two[2]))
    feed(2)
    feed(3)
    second_near_three = over_core(second[3])
    outward = (second[2].astype(F32) + second_near_three.astype(F32)).astype(BF)
    second_far = over_x(outward)

    far_grads = after((hidden[2], hidden[3], inner_grads[2], inner_grads[3]), outward)
    hidden[2], hidden[3], inner_grads[2], inner_grads[3] = far_grads
    outer_grad, inner_grad = (
        left + right for left, right in zip(first_grads, weight_grads((2, 3)))
    )
    feed_sum = Reduction("feed_sum", place, 2, *cut(place, (outer_grad, inner_grad)))

    second_far = after(second_far, feed_sum.kept)
    middle_grad, low, gain_two_grad = make_middle_grad(
        cotangent, middle, (second[0], second_near_one, second_far), gain_two.reshape(1, -1)
    )
    grads = [low, over_core(low), over_x(low)]
    outer_parts = outer_product(after([hidden[step] for step in range(4)], low), outer_weight)
    outer_near = [over_core(outer_parts[1]), over_core(outer_parts[3])]
    grads[2] = after(grads[2], outer_parts)
    grads.append(over_core(grads[2]))
    mark = feed_sum.step(grads[3])
    outward = after(outer_parts[2], mark).astype(F32) + outer_near[1].astype(F32)
    outward = outward.astype(BF)
    outer_far = over_x(outward)

    parts, lines, held, away = attend_backward(
        place, after(grads, outward), normed_one, output_weight, kept
    )
    mark = feed_sum.step(held)
    layer_output = make_layer_output(
        middle, (outer_parts[0], outer_near[0], after(outer_far, mark))
    )
    send, keep, rider, loaded = normed_grad(
        place,
        after(parts, layer_output),
        weights,
        gain_row,
        normed_one,
        gain_two_grad,
        lines,
        away,
    )
    attention_sum = Reduction("attention_sum", place, 1, held, loaded, rider)
    first_near = over_core(send)
    outward = (keep[1].astype(F32) + first_near[1].astype(F32)).astype(BF)
    first_far = over_x(outward)
    mark = attention_sum.step(outward)
    mark = feed_sum.step(mark)
    input_grad = make_input_grad(
        inputs, (keep, first_near, after(first_far, mark)), gain_row, middle_grad
    )
    mark = attention_sum.step(input_grad)
    small = attention_sum.rider
    gains = small[:8] + over_core(small[:8])
    mark = attention_sum.step(mark)
    outer_weight_grad, inner_weight_grad = feed_sum.finish(factor, 2, mark)
    gain_grads = (gains + over_x(gains))[:2]
    query_grad, key_grad, value_grad, output_weight_grad = attention_sum.finish(
        factor, 4, inner_weight_grad
    )

    slots = jnp.arange(table.shape[0], dtype=jnp.int32)
    offsets = jnp.arange(WIDE, dtype=jnp.int32) - (QT + NEAR - 1)
    chosen = buckets_of(offsets)[None, :] == slots[:, None]
    table_grad = jnp.sum(
        jnp.where(chosen[:, None, :], small[2 : 2 + head_count][None], 0.0), axis=2
    )
    return (
        layer_output,
        input_grad,
        query_grad.T,
        key_grad.T,
        value_grad.T,
        output_weight_grad,
        table_grad * factor,
        inner_weight_grad,
        outer_weight_grad,
        gain_grads * factor,
    )


def solution(mesh):
    return jax.shard_map(
        body,
        mesh=mesh,
        in_specs=(
            P(("dp", "tensor"), None),
            P("dp"),
            P(),
            P(None, "tensor"),
            P(None, "tensor"),
            P(None, "tensor"),
            P("tensor", None),
            P(None, "tensor"),
            P(),
            P(None, "tensor"),
            P("tensor", None),
            P(("dp", "tensor"), None),
        ),
        out_specs=(
            P(("dp", "tensor"), None),
            P(("dp", "tensor"), None),
            P(None, "tensor"),
            P(None, "tensor"),
            P(None, "tensor"),
            P("tensor", None),
            P(None, "tensor"),
            P(None, "tensor"),
            P("tensor", None),
            P(),
        ),
        check_vma=False,
    )
```

```python
import functools

import jax
import jax.numpy as jnp
from jax import lax
from jax.experimental import pallas as pl
from jax.experimental.pallas import tpu as pltpu
from jax.sharding import PartitionSpec as P

DH = 64
LONG = 1024
QT = 256
NEAR = 128
WIDE = 768
RIDER = 16
EDGES = (8, 12, 16, 23, 32, 46, 64, 91)
EPSILON = 1e-06
MASKED = -1000000000.0
BF = jnp.bfloat16
F32 = jnp.float32


def buckets_of(offset):
    distance = jnp.abs(offset)
    coarse = jnp.full(distance.shape, 7, jnp.int32)
    for boundary in EDGES:
        coarse = coarse + (distance >= boundary).astype(jnp.int32)
    bucket = jnp.where(distance < 8, distance, coarse)
    return bucket + jnp.where(offset > 0, 16, 0).astype(jnp.int32)


def dot(left, right, dims=((1,), (0,))):
    return lax.dot_general(left, right, (dims, ((), ())), preferred_element_type=F32)


ROWS_T = ((1,), (1,))
T_ROWS = ((0,), (0,))


FREE = pl.CostEstimate(flops=0, bytes_accessed=0, transcendentals=0)
LONG_KERNEL = pl.CostEstimate(flops=200_000_000_000, bytes_accessed=0, transcendentals=0)


def params(limit=30):
    return pltpu.CompilerParams(vmem_limit_bytes=limit * 1024 * 1024)


def struct(shape, dtype):
    return jax.ShapeDtypeStruct(shape, dtype)


def one(shape, *index):
    index = index + (0,) * (len(shape) - len(index))
    return pl.BlockSpec(shape, lambda i: index)


def call(kernel, name, outs, ins, operands, scratch=(), cost=FREE):
    spec = lambda item: item if isinstance(item, pl.BlockSpec) else one(item.shape)
    return pl.pallas_call(
        kernel,
        grid=(1,),
        out_shape=outs,
        in_specs=[spec(item) for item in ins],
        out_specs=tuple(one(o.shape) for o in outs),
        scratch_shapes=scratch,
        compiler_params=params(),
        cost_estimate=cost,
        name=name,
    )(*operands)


def vmem():
    return pl.BlockSpec(memory_space=pltpu.VMEM)


def smem():
    return pl.BlockSpec(memory_space=pltpu.SMEM)


def near_kernel(table_ref, near_ref):
    head_count = near_ref.shape[0]
    lane = lax.broadcasted_iota(jnp.int32, (8, WIDE), 1)
    bucket = buckets_of(lane - (QT + NEAR - 1))
    for head in range(head_count):
        line = jnp.zeros((8, WIDE), F32)
        for slot in range(table_ref.shape[0]):
            line = jnp.where(bucket == slot, table_ref[slot, head], line)
        rows = jnp.broadcast_to(line[:1], (QT, WIDE))
        turned = pltpu.roll(rows, WIDE - QT + 1, 1, stride=1, stride_axis=0)
        near_ref[head] = turned[:, : QT + 2 * NEAR]


def near_bias(table):
    head_count = table.shape[1]
    return pl.pallas_call(
        near_kernel,
        out_shape=jax.ShapeDtypeStruct((head_count, QT, QT + 2 * NEAR), F32),
        in_specs=[smem()],
        out_specs=vmem(),
        compiler_params=params(),
        name="near_bias",
    )(table)


def pieces_of(tile, keys):
    low = max(tile * QT - NEAR, 0)
    high = min(tile * QT + QT + NEAR, keys)
    return low, high, low - (tile * QT - NEAR)


def tiles_of(total):
    ranges = [(0, LONG)] + ([(LONG, total - LONG)] if total > LONG else [])
    return [
        (first + tile * QT, first, keys, tile)
        for first, keys in ranges
        for tile in range(keys // QT)
    ]


def stored_tile(spots, head, tile, prob, rest):
    row, first, keys, number = spots[tile]
    return (rest if first else prob).at[head, pl.ds(number * QT, QT), :]


def forward_kernel(
    place_ref,
    table_ref,
    block0,
    block1,
    block2,
    block3,
    gain_ref,
    query_weight_ref,
    key_weight_ref,
    value_weight_ref,
    near_ref,
    row_segment_ref,
    key_segment_ref,
    output_weight_ref,
    packed_ref,
    prob_out,
    rest_out,
    normed_out,
    send_ref,
    keep_ref,
    gathered,
    query,
    key,
    value,
    normed,
    prob,
    rest,
    weight,
    sems,
    normed_sem,
):
    head = pl.program_id(0)
    head_count = pl.num_programs(0)
    place = place_ref[0]
    for which, ref in enumerate((query_weight_ref, key_weight_ref, value_weight_ref)):
        weight[which * DH : which * DH + DH, :] = ref[...]
    blocks = (block0, block1, block2, block3)
    size = block0.shape[0]
    normed_copy = pltpu.make_async_copy(normed, normed_out, normed_sem)

    @pl.when(head == 0)
    def _():
        for step, block in enumerate(blocks):
            values = block[...].astype(F32)
            inverse = inverse_root(values)
            normed[step] = (values * inverse * gain_ref[...].astype(F32)).astype(BF)
        normed_copy.start()

    for step in range(4):
        row = pl.multiple_of((place ^ step) * size, size)
        rows = pl.ds(row, size)
        made = dot(normed[step], weight[...], ROWS_T).astype(BF)
        packed_ref[0, rows, : 3 * DH] = made
        query[rows, :] = made[:, :DH]
        key[rows, :] = made[:, DH : 2 * DH]
        value[rows, :] = made[:, 2 * DH :]
    total = query.shape[0]
    left_bias = table_ref[15, head]
    right_bias = table_ref[31, head]
    spots = tiles_of(total)

    def copy_of(which, tile):
        return pltpu.make_async_copy(
            stored_tile(spots, which, tile, prob, rest),
            stored_tile(spots, which, tile, prob_out, rest_out),
            sems.at[which, tile],
        )

    for index, (row, first, keys, tile) in enumerate(spots):
        low, high, lane = pieces_of(tile, keys)
        rows = slice(row, row + QT)
        local = slice(tile * QT, tile * QT + QT)
        store = rest if first else prob
        scores = dot(query[rows, :], key[first : first + keys, :], ROWS_T)
        parts = []
        if low > 0:
            parts.append((0, low, scores[:, :low] + left_bias))
        parts.append((low, high, scores[:, low:high] + near_ref[0, :, lane : lane + high - low]))
        if high < keys:
            parts.append((high, keys, scores[:, high:] + right_bias))
        if first:
            row_segment = row_segment_ref[local, :]
            parts = [
                (a, b, jnp.where(row_segment == key_segment_ref[:, a:b], part, MASKED))
                for a, b, part in parts
            ]
        peak = functools.reduce(
            jnp.maximum, [jnp.max(part, axis=1, keepdims=True) for a, b, part in parts]
        )
        parts = [(a, b, jnp.exp(part - peak)) for a, b, part in parts]
        whole = sum(jnp.sum(part, axis=1, keepdims=True) for a, b, part in parts)
        share = 1.0 / whole
        for a, b, part in parts:
            store[head, local, a:b] = (part * share).astype(BF)
        made = dot(store[head, local, :], value[first : first + keys, :]).astype(BF)
        packed_ref[0, rows, 3 * DH :] = made
        copy_of(head, index).start()
    for which in range(gathered.shape[1] // DH):

        @pl.when(head == which)
        def _():
            gathered[:, which * DH : which * DH + DH] = packed_ref[0, :, 3 * DH :]

    @pl.when(head == head_count - 1)
    def _():
        for step in (1, 3, 2, 0):
            row = pl.multiple_of((place ^ step) * size, size)
            made = dot(gathered[pl.ds(row, size), :], output_weight_ref[...]).astype(BF)
            out = send_ref if step & 1 else keep_ref
            out[step >> 1] = made
        normed_copy.wait()
        for which in range(gathered.shape[1] // DH):
            for index in range(len(spots)):
                copy_of(which, index).wait()


def attend_forward(place, table, blocks, gain, weights, near, row_segment, key_segment, output_weight):
    size, width = blocks[0].shape
    head_count = near.shape[0]
    total = 4 * size
    rest = total - LONG
    by_head = lambda *shape: pl.BlockSpec((1, *shape), lambda h: (h, *(0 for _ in shape)))
    whole = lambda *shape: pl.BlockSpec(shape, lambda h: tuple(0 for _ in shape))
    apart = pl.BlockSpec(memory_space=pl.ANY)
    return pl.pallas_call(
        forward_kernel,
        grid=(head_count,),
        out_shape=(
            struct((head_count, total, 4 * DH), BF),
            struct((head_count, LONG, LONG), BF),
            struct((head_count, rest, rest), BF),
            struct((4, size, width), BF),
            struct((2, size, width), BF),
            struct((2, size, width), BF),
            struct((total, head_count * DH), BF),
        ),
        in_specs=[
            smem(),
            smem(),
            *(whole(size, width) for _ in range(4)),
            whole(1, width),
            *(pl.BlockSpec((DH, width), lambda h: (h, 0)) for _ in range(3)),
            by_head(QT, QT + 2 * NEAR),
            whole(rest, 1),
            whole(1, rest),
            whole(head_count * DH, width),
        ],
        out_specs=(
            by_head(total, 4 * DH),
            apart,
            apart,
            apart,
            whole(2, size, width),
            whole(2, size, width),
            whole(total, head_count * DH),
        ),
        scratch_shapes=[
            pltpu.VMEM((total, DH), BF),
            pltpu.VMEM((total, DH), BF),
            pltpu.VMEM((total, DH), BF),
            pltpu.VMEM((4, size, width), BF),
            pltpu.VMEM((head_count, LONG, LONG), BF),
            pltpu.VMEM((head_count, rest, rest), BF),
            pltpu.VMEM((3 * DH, width), BF),
            pltpu.SemaphoreType.DMA((head_count, total // QT)),
            pltpu.SemaphoreType.DMA,
        ],
        compiler_params=params(56),
        cost_estimate=LONG_KERNEL,
        name="attend_forward",
    )(place, table, *blocks, gain, *weights, near, row_segment, key_segment, output_weight)


def backward_kernel(
    place_ref,
    grad0,
    grad1,
    grad2,
    grad3,
    normed_in,
    output_weight_ref,
    packed_ref,
    gathered_ref,
    prob_in,
    rest_in,
    parts_ref,
    line_ref,
    kept_ref,
    away_ref,
    *more_refs,
):
    (
        normed,
        prob,
        rest,
        query,
        key,
        value,
        context,
        turned,
        context_grad,
        near_total,
        far_total,
        key_total,
        value_total,
        sums,
        sems,
        normed_sem,
    ) = more_refs
    head = pl.program_id(0)
    head_count = pl.num_programs(0)
    place = place_ref[0]
    bit = place_ref[1] & 1
    size = normed.shape[1]
    total = query.shape[0]
    spots = tiles_of(total)
    blocks = [pl.multiple_of((place ^ step) * size, size) for step in range(4)]
    normed_copy = pltpu.make_async_copy(normed_in, normed, normed_sem)

    def copy_of(which, tile):
        return pltpu.make_async_copy(
            stored_tile(spots, which, tile, prob_in, rest_in),
            stored_tile(spots, which, tile, prob, rest),
            sems.at[which, tile],
        )

    @pl.when(head == 0)
    def _():
        for which in range(prob.shape[0]):
            for index in range(len(spots)):
                copy_of(which, index).start()
            if which == 0:
                normed_copy.start()

    query[...] = packed_ref[0, :, :DH]
    key[...] = packed_ref[0, :, DH : 2 * DH]
    value[...] = packed_ref[0, :, 2 * DH : 3 * DH]
    context[...] = packed_ref[0, :, 3 * DH :]
    turned[...] = key[...].T
    whole = sums.shape[0] // 4

    @pl.when(head == 0)
    def _():
        output_grad = 0.0
        for row, grad in zip(blocks, (grad0, grad1, grad2, grad3)):
            rows = pl.ds(row, size)
            made = dot(grad[...], output_weight_ref[...], ROWS_T).astype(BF)
            for which in range(context_grad.shape[0]):
                context_grad[which, rows, :] = made[:, which * DH : which * DH + DH]
            output_grad += dot(gathered_ref[rows, :], grad[...], T_ROWS)
        sums[3 * whole :, :] = output_grad

    near_total[...] = jnp.zeros_like(near_total)
    far_total[...] = jnp.zeros_like(far_total)

    for index, (row, first, keys, tile) in enumerate(spots):
        low, high, lane = pieces_of(tile, keys)
        rows = slice(row, row + QT)
        span = slice(first, first + keys)
        local = slice(tile * QT, tile * QT + QT)
        grads = context_grad[head, rows, :]
        prob_grad = dot(grads, value[span, :], ROWS_T)
        row_dot = jnp.sum(
            grads.astype(F32) * context[rows, :].astype(F32), axis=1, keepdims=True
        )
        copy_of(head, index).wait()
        taken = (rest if first else prob)[head, local, :]
        score_grad = taken.astype(F32) * (prob_grad - row_dot)
        low_grad = score_grad.astype(BF)
        near_total[:, lane : lane + high - low] += score_grad[:, low:high]
        for side, (a, b) in enumerate(((0, low), (high, keys))):
            if b > a:
                far_total[side] += sum(score_grad[:, c : c + 128] for c in range(a, b, 128))
        parts_ref[0, :DH, rows] = dot(turned[:, span], low_grad, ROWS_T).astype(BF)
        value_part = dot(grads, taken, T_ROWS)
        key_part = dot(query[rows, :], low_grad, T_ROWS)
        if tile == 0:
            value_total[:, span] = value_part
            key_total[:, span] = key_part
        else:
            value_total[:, span] += value_part
            key_total[:, span] += key_part

    padded = jnp.concatenate(
        [near_total[...], jnp.zeros((QT, WIDE - near_total.shape[1]), F32)], axis=1
    )
    count = QT
    while count > 1:
        count //= 2
        padded = padded[:count] + pltpu.roll(padded[count:], WIDE - count, 1)
    line = pltpu.roll(padded, QT - 1, 1)
    lanes = lax.broadcasted_iota(jnp.int32, line.shape, 1)
    line = jnp.where(lanes == 0, jnp.sum(far_total[0]), line)
    line_ref[0] = jnp.where(lanes == WIDE - 1, jnp.sum(far_total[1]), line)

    parts_ref[0, DH : 2 * DH, :] = key_total[...].astype(BF)
    parts_ref[0, 2 * DH :, :] = value_total[...].astype(BF)

    @pl.when(head == 0)
    def _():
        normed_copy.wait()

    made = sum(
        dot(parts_ref[0, :, pl.ds(row, size)], normed[step])
        for step, row in enumerate(blocks)
    )
    for which in range(3):
        row = pl.multiple_of(which * whole + head * DH, DH)
        sums[pl.ds(row, DH), :] = made[which * DH : which * DH + DH]

    @pl.when(head == head_count - 1)
    def _():
        half = kept_ref.shape[0]
        for flip, out in enumerate((kept_ref, away_ref)):
            row = pl.multiple_of((bit ^ flip) * half, half)
            out[...] = sums[pl.ds(row, half), :].astype(out.dtype)


def attend_backward(place, grads, normed, output_weights, kept):
    packed, prob, rest, gathered = kept
    _, size, width = normed.shape
    head_count, total, _ = packed.shape
    rows = 4 * DH * head_count
    by_head = lambda *shape: pl.BlockSpec((1, *shape), lambda h: (h, *(0 for _ in shape)))
    whole = lambda *shape: pl.BlockSpec(shape, lambda h: tuple(0 for _ in shape))
    apart = pl.BlockSpec(memory_space=pl.ANY)
    return pl.pallas_call(
        backward_kernel,
        grid=(head_count,),
        out_shape=(
            struct((head_count, 3 * DH, total), BF),
            struct((head_count, 1, WIDE), F32),
            struct((rows // 2, width), F32),
            struct((rows // 2, width), BF),
        ),
        in_specs=[
            smem(),
            *(whole(size, width) for _ in range(4)),
            apart,
            whole(head_count * DH, width),
            by_head(total, 4 * DH),
            whole(total, head_count * DH),
            apart,
            apart,
        ],
        out_specs=(
            by_head(3 * DH, total),
            by_head(1, WIDE),
            whole(rows // 2, width),
            whole(rows // 2, width),
        ),
        scratch_shapes=[
            pltpu.VMEM(normed.shape, BF),
            pltpu.VMEM(prob.shape, BF),
            pltpu.VMEM(rest.shape, BF),
            *(pltpu.VMEM((total, DH), BF) for _ in range(4)),
            pltpu.VMEM((DH, total), BF),
            pltpu.VMEM((head_count, total, DH), BF),
            pltpu.VMEM((QT, QT + 2 * NEAR), F32),
            pltpu.VMEM((2, QT, 128), F32),
            pltpu.VMEM((DH, total), F32),
            pltpu.VMEM((DH, total), F32),
            pltpu.VMEM((rows, width), F32),
            pltpu.SemaphoreType.DMA((head_count, total // QT)),
            pltpu.SemaphoreType.DMA,
        ],
        compiler_params=params(40),
        cost_estimate=LONG_KERNEL,
        name="attend_backward",
    )(place, *grads, normed, output_weights, packed, gathered, prob, rest)


def normed_grad_kernel(
    place_ref,
    parts_ref,
    query_weight_ref,
    key_weight_ref,
    value_weight_ref,
    gain_ref,
    normed_ref,
    gain_two_ref,
    line_ref,
    away_ref,
    send_ref,
    keep_ref,
    rider_ref,
    loaded_ref,
):
    place = place_ref[0]
    size = normed_ref.shape[1]
    gain_grad = 0.0
    weights = (query_weight_ref, key_weight_ref, value_weight_ref)
    for step in range(4):
        row = pl.multiple_of((place ^ step) * size, size)
        made = 0.0
        for head in range(parts_ref.shape[0]):
            weight = jnp.concatenate([ref[head * DH : head * DH + DH, :] for ref in weights])
            made += dot(parts_ref[head, :, pl.ds(row, size)], weight, T_ROWS)
        out = send_ref if step & 1 else keep_ref
        out[step >> 1] = made.astype(BF)
        gain_grad += jnp.sum(made * normed_ref[step].astype(F32), axis=0, keepdims=True)
    rider_ref[...] = jnp.zeros_like(rider_ref)
    rider_ref[0:1, :] = gain_grad / gain_ref[...].astype(F32)
    rider_ref[1:2, :] = gain_two_ref[...]
    for head in range(line_ref.shape[0]):
        rider_ref[2 + head : 3 + head, :] = line_ref[head]
    half = away_ref.shape[0]
    loaded_ref[:half, :] = away_ref[...]
    loaded_ref[half:, :] = rider_ref[...].astype(BF)


def normed_grad(place, parts, weights, gain, normed, gain_two_grad, lines, away):
    _, size, width = normed.shape
    operands = (parts, *weights, gain, normed, gain_two_grad, lines, away)
    return call(
        normed_grad_kernel,
        "normed_grad",
        (
            struct((2, size, width), BF),
            struct((2, size, width), BF),
            struct((RIDER, width), F32),
            struct((away.shape[0] + RIDER, width), BF),
        ),
        (smem(), *operands),
        (place, *operands),
        cost=LONG_KERNEL,
    )


def inverse_root(values):
    return lax.rsqrt(jnp.mean(values * values, axis=-1, keepdims=True) + EPSILON)


def norm_input_grad(values, inverse, gains, upstream):
    scaled = upstream * gains
    projection = jnp.mean(scaled * values, axis=-1, keepdims=True)
    return inverse * scaled - values * (inverse * inverse * inverse) * projection


def middle_grad_kernel(
    cotangent_ref, middle_ref, own_ref, near_ref, far_ref, gain_ref, grad_ref, low_ref, gain_grad_ref
):
    upstream = own_ref[...].astype(F32) + near_ref[...].astype(F32) + far_ref[...].astype(F32)
    values = middle_ref[...]
    inverse = inverse_root(values)
    grad = cotangent_ref[...].astype(F32) + norm_input_grad(
        values, inverse, gain_ref[...].astype(F32), upstream
    )
    grad_ref[...] = grad
    low_ref[...] = grad.astype(BF)
    gain_grad_ref[...] = jnp.sum(upstream * values * inverse, axis=0, keepdims=True)


def make_middle_grad(cotangent, middle, sums, gain):
    shape = middle.shape
    operands = (cotangent, middle, *sums, gain)
    return call(
        middle_grad_kernel,
        "middle_grad",
        (struct(shape, F32), struct(shape, BF), struct((1, shape[1]), F32)),
        operands,
        operands,
    )


def input_grad_kernel(input_ref, own_ref, near_ref, far_ref, gain_ref, middle_ref, out_ref):
    upstream = own_ref[0].astype(F32) + near_ref[0].astype(F32) + far_ref[...].astype(F32)
    values = input_ref[...].astype(F32)
    out_ref[...] = middle_ref[...] + norm_input_grad(
        values, inverse_root(values), gain_ref[...], upstream
    )


def make_input_grad(inputs, sums, gain, middle_grad):
    first = one((1, *inputs.shape))
    return call(
        input_grad_kernel,
        "input_grad",
        (struct(inputs.shape, F32),),
        (inputs, first, first, sums[2], gain, middle_grad),
        (inputs, *sums, gain, middle_grad),
    )[0]


def layer_output_kernel(middle_ref, own_ref, near_ref, far_ref, out_ref):
    own, near, far = (ref[...].astype(F32) for ref in (own_ref, near_ref, far_ref))
    out_ref[...] = (middle_ref[...] + (own + near + far)).astype(BF)


def make_layer_output(middle, sums):
    operands = (middle, *sums)
    return call(
        layer_output_kernel, "layer_output", (struct(middle.shape, BF),), operands, operands
    )[0]


def outer_kernel(weight_ref, *refs):
    hidden_refs, out_refs = refs[:4], refs[4:]
    for hidden, out in zip(hidden_refs, out_refs):
        out[...] = dot(hidden[...], weight_ref[...]).astype(BF)


def outer_product(hidden, weight):
    operands = (weight, *hidden)
    shape = struct((hidden[0].shape[0], weight.shape[1]), BF)
    return call(outer_kernel, "outer", (shape,) * 4, operands, operands, cost=LONG_KERNEL)


def after(values, *others):
    return lax.optimization_barrier((values, others))[0]


def across(values, axis, flip):
    count = lax.axis_size(axis)
    return lax.ppermute(values, axis, [(i, i ^ flip) for i in range(count)])


def over_core(values):
    return across(values, "tensor", 1)


def over_x(values):
    return across(values, "tensor", 2)


def usual():
    return lax.axis_size("dp") == 8


def split_kernel(place_ref, *refs):
    kept_ref, came_ref, *refs = refs
    riders, refs = refs[:-4], refs[-4:]
    own_ref, *away_refs = refs
    size = own_ref.shape[0]
    spot = place_ref[1] >> 1
    if riders:
        rider_ref, total_ref = riders
        half = kept_ref.shape[0]
        total_ref[...] = rider_ref[...] + came_ref[half:, :].astype(F32)
        for out in away_refs:
            out[size:, :] = total_ref[...].astype(BF)
    for flip, out in enumerate((own_ref, *away_refs)):
        rows = pl.ds(pl.multiple_of((spot ^ flip) * size, size), size)
        out[:size, :] = (kept_ref[rows, :] + came_ref[rows, :].astype(F32)).astype(out.dtype)


def four_kernel(own_ref, came0, came1, came2, *refs):
    *riders, out_ref = refs
    size = own_ref.shape[0]
    total = own_ref[...]
    for came in (came0, came1, came2):
        total += came[:size, :].astype(F32)
    out_ref[...] = total.astype(BF)
    if riders:
        rider_ref, sum_ref = riders
        total = rider_ref[...]
        for came in (came0, came1, came2):
            total += came[size:, :].astype(F32)
        sum_ref[...] = total


def pair_kernel(place_ref, own_ref, came_ref, out_ref):
    size = own_ref.shape[0]
    bit = (place_ref[1] >> 2) & 1
    for flip, ref in enumerate((own_ref, came_ref)):
        out_ref[pl.ds(pl.multiple_of((bit ^ flip) * size, size), size), :] = ref[...]


def half_kernel(place_ref, pair_ref, came_ref, out_ref):
    size = pair_ref.shape[0] // 2
    bit = (place_ref[1] >> 1) & 1
    for flip, ref in enumerate((pair_ref, came_ref)):
        for which in range(2):
            row = pl.multiple_of(((bit ^ flip) + 2 * which) * size, size)
            out_ref[pl.ds(row, size), :] = ref[which * size : which * size + size, :]


def join_kernel(place_ref, own_ref, came0, came1, came2, out_ref):
    size = own_ref.shape[0]
    spot = place_ref[1] >> 1
    for flip, ref in enumerate((own_ref, came0, came1, came2)):
        out_ref[pl.ds(pl.multiple_of((spot ^ flip) * size, size), size), :] = ref[...]


def whole_kernel(factor, pieces, place_ref, own_ref, came_ref, *refs):
    *out_refs, whole = refs
    part = own_ref.shape[0] // pieces
    bit = place_ref[1] & 1
    for flip, ref in enumerate((own_ref, came_ref)):
        for piece in range(pieces):
            row = pl.multiple_of((2 * piece + (bit ^ flip)) * part, part)
            whole[pl.ds(row, part), :] = ref[piece * part : piece * part + part, :]
    rows = whole.shape[0] // len(out_refs)
    for index, out in enumerate(out_refs):
        out[...] = whole[index * rows : index * rows + rows, :].astype(F32) * factor


def cut_kernel(place_ref, *refs):
    whole_refs, kept_ref, away_ref = refs[:-2], refs[-2], refs[-1]
    bit = place_ref[1] & 1
    half = whole_refs[0].shape[0] // 2
    for index, ref in enumerate(whole_refs):
        here = slice(index * half, index * half + half)
        for flip, out in enumerate((kept_ref, away_ref)):
            rows = pl.ds(pl.multiple_of((bit ^ flip) * half, half), half)
            out[here, :] = ref[rows, :].astype(out.dtype)


def cut(place, arrays):
    rows, width = arrays[0].shape
    shape = (len(arrays) * rows // 2, width)
    return call(
        cut_kernel, "cut", (struct(shape, F32), struct(shape, BF)), (smem(), *arrays), (place, *arrays)
    )


class Reduction:
    def __init__(self, name, place, pieces, kept, away, rider=None):
        self.name, self.place, self.pieces, self.rider = name, place, pieces, rider
        self.rows, self.width = 2 * kept.shape[0], kept.shape[1]
        self.stage = 0
        self.count = lax.axis_size("dp")
        self.halves = (kept, away[: kept.shape[0]])
        self.kept = kept
        if self.count == 8:
            self.came = across(away, "dp", 1)

    def step(self, *others):
        self.stage += 1
        if self.count != 8:
            if self.stage == 1 and self.rider is not None:
                self.rider = lax.psum(self.rider, "dp")
            return self.kept
        width = self.width
        name = f"{self.name}_{self.stage}"
        riders = () if self.rider is None else (self.rider,)
        also = tuple(struct(item.shape, F32) for item in riders)
        if self.stage == 1:
            size = self.rows // 8
            far = size + sum(item.shape[0] for item in riders)
            operands = (self.kept, after(self.came, *others), *riders)
            *riders, own, a, b, c = call(
                split_kernel,
                name,
                (*also, struct((size, width), F32), *(struct((far, width), BF) for _ in range(3))),
                (smem(), *operands),
                (self.place, *operands),
                cost=FREE if self.rider is None else LONG_KERNEL,
            )
            self.kept = own
            self.came = [across(item, "dp", 2 * flip) for flip, item in enumerate((a, b, c), 1)]
            self.rider = riders[0] if riders else None
            return own
        if self.stage == 2:
            operands = (self.kept, *after(self.came, *others), *riders)
            *riders, low = call(
                four_kernel, name, (*also, struct(self.kept.shape, BF)), operands, operands
            )
            self.kept = low
            if riders:
                self.came = [across(low, "dp", 2 * flip) for flip in range(1, 4)]
                self.rider = riders[0]
            else:
                self.came = across(low, "dp", 4)
            return low
        if self.rider is None:
            flip, kernel = {3: (2, pair_kernel), 4: (1, half_kernel)}[self.stage]
            operands = (self.kept, after(self.came, *others))
            rows = 2 * self.kept.shape[0]
            self.kept = call(
                kernel,
                name,
                (struct((rows, width), BF),),
                (smem(), *operands),
                (self.place, *operands),
                cost=LONG_KERNEL if self.stage == 3 else FREE,
            )[0]
            self.came = across(self.kept, "dp", flip)
            return self.kept
        if self.stage == 3:
            operands = (self.kept, *after(self.came, *others))
            half = call(
                join_kernel,
                name,
                (struct((self.rows // 2, width), BF),),
                (smem(), *operands),
                (self.place, *operands),
            )[0]
            self.kept = half
            self.came = across(half, "dp", 1)
            return half
        raise ValueError("over")

    def finish(self, factor, count, *others):
        own, came = self.kept, self.came if self.count == 8 else None
        if self.count != 8:
            kept, away = self.halves
            bit = lax.axis_index("dp") & 1
            away = away.astype(F32)
            first = jnp.where(bit == 0, kept, away)
            second = jnp.where(bit == 0, away, kept)
            total = sum_over_dp(jnp.concatenate([first, second])).astype(BF)
            half = kept.shape[0]
            own = lax.dynamic_slice_in_dim(total, bit * half, half)
            came = lax.dynamic_slice_in_dim(total, (1 - bit) * half, half)
        operands = (own, after(came, *others))
        width = self.width
        return call(
            functools.partial(whole_kernel, factor, self.pieces),
            self.name,
            (struct((self.rows // count, width), F32),) * count,
            (smem(), *operands),
            (self.place, *operands),
            (pltpu.VMEM((self.rows, width), BF),),
        )


def sum_over_dp(values):
    count = lax.axis_size("dp")
    if count & (count - 1) or values.shape[0] % count:
        return lax.psum(values, "dp")
    index = lax.axis_index("dp")
    bits = count.bit_length() - 1
    for bit in range(bits):
        half = values.shape[0] // 2
        mine = (index >> bit) & 1
        keep = lax.dynamic_slice_in_dim(values, mine * half, half)
        away = lax.dynamic_slice_in_dim(values, (1 - mine) * half, half)
        values = keep + across(away.astype(BF), "dp", 1 << bit).astype(F32)
    values = values.astype(BF)
    for bit in reversed(range(bits)):
        mine = (index >> bit) & 1
        came = across(values, "dp", 1 << bit)
        first = jnp.where(mine == 0, values, came)
        second = jnp.where(mine == 0, came, values)
        values = jnp.concatenate([first, second])
    return values.astype(F32)


ROOT = 0.7978845608028654
CUBE = 0.044715


def gate(value):
    square = value * value
    tanh = jnp.tanh(ROOT * value * (1.0 + CUBE * square))
    half = 0.5 * (1.0 + tanh)
    slope = half + 0.5 * ROOT * value * (1.0 - tanh * tanh) * (1.0 + 3.0 * CUBE * square)
    return value * half, slope


def body(
    inputs,
    segments,
    first_gain,
    query_weight,
    lookup_projection,
    value_weight,
    output_weight,
    bucket_bias_table,
    second_gain,
    inner_weight,
    outer_weight,
    cotangent,
):
    total = segments.shape[0]
    size, width = inputs.shape
    head_count = query_weight.shape[1] // DH
    factor = float(total * lax.axis_size("dp")) ** (-0.5)

    far, near_block = over_x(inputs), over_core(inputs)
    place = jnp.stack([lax.axis_index("tensor"), lax.axis_index("dp")]).astype(jnp.int32)
    gain_one = first_gain.astype(F32)
    gain_two = second_gain.astype(F32)
    gain_row = gain_one.reshape(1, -1)
    table = bucket_bias_table.astype(F32)
    weights = (query_weight.T, lookup_projection.T, value_weight.T)
    near = near_bias(table)
    row_segment = segments[LONG:].reshape(-1, 1)
    key_segment = segments[LONG:].reshape(1, -1)
    norm_input = inputs.astype(F32)
    inverse_one = inverse_root(norm_input)
    far = after(far, near, row_segment, place, gain_row, inverse_one)
    blocks = (inputs, near_block, far, over_core(far))
    cot_far = over_x(after(cotangent, far))
    cot_near = over_core(after(cotangent, far))

    *kept, normed_one, send, keep, gathered = attend_forward(
        place, table, blocks, gain_row, weights, near, row_segment, key_segment, output_weight
    )
    kept.append(gathered)
    cot_far = after(cot_far, keep)
    send = after(send, cot_far)
    near_sums = [None, over_core(send[1])]
    near_sums[0] = over_core(after(send[0], near_sums[1]))
    outward = (keep[1].astype(F32) + near_sums[1].astype(F32)).astype(BF)
    far_sum = over_x(outward)
    cot_far = after(cot_far, outward)
    cotangents = (cotangent, cot_near, cot_far, over_core(cot_far))
    hidden_grads = {}
    for step in (2, 3):
        hidden_grads[step] = dot(cotangents[step], outer_weight, ROWS_T)
    far_sum = after(far_sum, hidden_grads)

    middle = norm_input + (
        keep[0].astype(F32) + near_sums[0].astype(F32) + far_sum.astype(F32)
    )
    inverse_two = inverse_root(middle)
    low = (middle * inverse_two * gain_two).astype(BF)
    normed_two = [low, over_core(low), over_x(low)]

    hidden, inner_grads, second = {}, {}, {}

    def feed(step):
        values, slope = gate(dot(normed_two[step], inner_weight))
        hidden[step] = values.astype(BF)
        if step not in hidden_grads:
            hidden_grads[step] = dot(cotangents[step], outer_weight, ROWS_T)
        inner_grads[step] = (hidden_grads[step] * slope).astype(BF)
        second[step] = dot(inner_grads[step], inner_weight, ROWS_T).astype(BF)

    def weight_grads(steps):
        outer = sum(dot(hidden[step], cotangents[step], T_ROWS) for step in steps)
        inner = sum(dot(normed_two[step], inner_grads[step], T_ROWS) for step in steps)
        return outer, inner

    feed(0)
    feed(1)
    second_near_one = over_core(second[1])
    first_grads = weight_grads((0, 1))
    normed_two[2] = after(normed_two[2], second, first_grads)
    normed_two.append(over_core(normed_two[2]))
    feed(2)
    normed_two[3] = after(normed_two[3], second[2])
    feed(3)
    second_near_three = over_core(second[3])
    outward = (second[2].astype(F32) + second_near_three.astype(F32)).astype(BF)
    second_far = over_x(outward)

    far_grads = after((hidden[2], hidden[3], inner_grads[2], inner_grads[3]), outward)
    hidden[2], hidden[3], inner_grads[2], inner_grads[3] = far_grads
    outer_grad, inner_grad = (
        left + right for left, right in zip(first_grads, weight_grads((2, 3)))
    )
    feed_sum = Reduction("feed_sum", place, 2, *cut(place, (outer_grad, inner_grad)))

    second_far = after(second_far, feed_sum.kept)
    middle_grad, low, gain_two_grad = make_middle_grad(
        cotangent, middle, (second[0], second_near_one, second_far), gain_two.reshape(1, -1)
    )
    grads = [low, over_core(low), over_x(low)]
    outer_parts = outer_product(after([hidden[step] for step in range(4)], low), outer_weight)
    outer_near = [over_core(outer_parts[1]), over_core(outer_parts[3])]
    grads[2] = after(grads[2], outer_parts)
    grads.append(over_core(grads[2]))
    mark = feed_sum.step(grads[3])
    outward = after(outer_parts[2], mark).astype(F32) + outer_near[1].astype(F32)
    outward = outward.astype(BF)
    outer_far = over_x(outward)

    parts, lines, held, away = attend_backward(
        place, after(grads, outward), normed_one, output_weight, kept
    )
    mark = feed_sum.step(held)
    send, keep, rider, loaded = normed_grad(
        place, after(parts, mark), weights, gain_row, normed_one, gain_two_grad, lines, away
    )
    attention_sum = Reduction("attention_sum", place, 1, held, loaded, rider)
    layer_output = make_layer_output(
        middle, (outer_parts[0], outer_near[0], after(outer_far, keep))
    )
    first_near = over_core(send)
    mark = feed_sum.step(layer_output)
    mark = attention_sum.step(mark)
    outward = keep[1].astype(F32) + after(first_near[1], mark).astype(F32)
    outward = outward.astype(BF)
    first_far = over_x(outward)
    mark = feed_sum.step(outward)
    input_grad = make_input_grad(
        inputs, (keep, first_near, after(first_far, mark)), gain_row, middle_grad
    )
    mark = attention_sum.step(input_grad)
    small = attention_sum.rider
    gains = small[:8] + over_core(small[:8])
    mark = attention_sum.step(mark)
    outer_weight_grad, inner_weight_grad = feed_sum.finish(factor, 2, mark)
    gain_grads = (gains + over_x(gains))[:2]
    query_grad, key_grad, value_grad, output_weight_grad = attention_sum.finish(
        factor, 4, inner_weight_grad
    )

    slots = jnp.arange(table.shape[0], dtype=jnp.int32)
    offsets = jnp.arange(WIDE, dtype=jnp.int32) - (QT + NEAR - 1)
    chosen = buckets_of(offsets)[None, :] == slots[:, None]
    table_grad = jnp.sum(
        jnp.where(chosen[:, None, :], small[2 : 2 + head_count][None], 0.0), axis=2
    )
    return (
        layer_output,
        input_grad,
        query_grad.T,
        key_grad.T,
        value_grad.T,
        output_weight_grad,
        table_grad * factor,
        inner_weight_grad,
        outer_weight_grad,
        gain_grads * factor,
    )


def solution(mesh):
    return jax.shard_map(
        body,
        mesh=mesh,
        in_specs=(
            P(("dp", "tensor"), None),
            P("dp"),
            P(),
            P(None, "tensor"),
            P(None, "tensor"),
            P(None, "tensor"),
            P("tensor", None),
            P(None, "tensor"),
            P(),
            P(None, "tensor"),
            P("tensor", None),
            P(("dp", "tensor"), None),
        ),
        out_specs=(
            P(("dp", "tensor"), None),
            P(("dp", "tensor"), None),
            P(None, "tensor"),
            P(None, "tensor"),
            P(None, "tensor"),
            P("tensor", None),
            P(None, "tensor"),
            P(None, "tensor"),
            P("tensor", None),
            P(),
        ),
        check_vma=False,
    )
```

```python
import functools

import jax
import jax.numpy as jnp
from jax import lax
from jax.experimental import pallas as pl
from jax.experimental.pallas import tpu as pltpu
from jax.sharding import PartitionSpec as P

DH = 64
LONG = 1024
QT = 256
NEAR = 128
WIDE = 768
RIDER = 16
EDGES = (8, 12, 16, 23, 32, 46, 64, 91)
EPSILON = 1e-06
MASKED = -1000000000.0
BF = jnp.bfloat16
F32 = jnp.float32


def buckets_of(offset):
    distance = jnp.abs(offset)
    coarse = jnp.full(distance.shape, 7, jnp.int32)
    for boundary in EDGES:
        coarse = coarse + (distance >= boundary).astype(jnp.int32)
    bucket = jnp.where(distance < 8, distance, coarse)
    return bucket + jnp.where(offset > 0, 16, 0).astype(jnp.int32)


def dot(left, right, dims=((1,), (0,))):
    return lax.dot_general(left, right, (dims, ((), ())), preferred_element_type=F32)


ROWS_T = ((1,), (1,))
T_ROWS = ((0,), (0,))


FREE = pl.CostEstimate(flops=0, bytes_accessed=0, transcendentals=0)
LONG_KERNEL = pl.CostEstimate(flops=200_000_000_000, bytes_accessed=0, transcendentals=0)


def params(limit=30):
    return pltpu.CompilerParams(vmem_limit_bytes=limit * 1024 * 1024)


def struct(shape, dtype):
    return jax.ShapeDtypeStruct(shape, dtype)


def one(shape, *index):
    index = index + (0,) * (len(shape) - len(index))
    return pl.BlockSpec(shape, lambda i: index)


def call(kernel, name, outs, ins, operands, scratch=(), cost=FREE):
    spec = lambda item: item if isinstance(item, pl.BlockSpec) else one(item.shape)
    return pl.pallas_call(
        kernel,
        grid=(1,),
        out_shape=outs,
        in_specs=[spec(item) for item in ins],
        out_specs=tuple(one(o.shape) for o in outs),
        scratch_shapes=scratch,
        compiler_params=params(),
        cost_estimate=cost,
        name=name,
    )(*operands)


def vmem():
    return pl.BlockSpec(memory_space=pltpu.VMEM)


def smem():
    return pl.BlockSpec(memory_space=pltpu.SMEM)


def near_kernel(table_ref, segment_ref, near_ref, column_ref):
    head_count = near_ref.shape[0]
    line = segment_ref[...].astype(F32)
    column_ref[...] = jnp.broadcast_to(line, (column_ref.shape[1], line.shape[1])).T
    lane = lax.broadcasted_iota(jnp.int32, (8, WIDE), 1)
    bucket = buckets_of(lane - (QT + NEAR - 1))
    for head in range(head_count):
        line = jnp.zeros((8, WIDE), F32)
        for slot in range(table_ref.shape[0]):
            line = jnp.where(bucket == slot, table_ref[slot, head], line)
        rows = jnp.broadcast_to(line[:1], (QT, WIDE))
        turned = pltpu.roll(rows, WIDE - QT + 1, 1, stride=1, stride_axis=0)
        near_ref[head] = turned[:, : QT + 2 * NEAR]


def near_bias(table, segments):
    head_count = table.shape[1]
    return pl.pallas_call(
        near_kernel,
        out_shape=(
            struct((head_count, QT, QT + 2 * NEAR), F32),
            struct((segments.shape[1], 128), F32),
        ),
        in_specs=[smem(), vmem()],
        out_specs=(vmem(), vmem()),
        compiler_params=params(),
        name="near_bias",
    )(table, segments)


def pieces_of(tile, keys):
    low = max(tile * QT - NEAR, 0)
    high = min(tile * QT + QT + NEAR, keys)
    return low, high, low - (tile * QT - NEAR)


def tiles_of(total):
    ranges = [(0, LONG)] + ([(LONG, total - LONG)] if total > LONG else [])
    return [
        (first + tile * QT, first, keys, tile)
        for first, keys in ranges
        for tile in range(keys // QT)
    ]


def stored_tile(spots, head, tile, prob, rest):
    row, first, keys, number = spots[tile]
    return (rest if first else prob).at[head, pl.ds(number * QT, QT), :]


def forward_kernel(
    place_ref,
    table_ref,
    block0,
    block1,
    block2,
    block3,
    gain_ref,
    query_weight_ref,
    key_weight_ref,
    value_weight_ref,
    near_ref,
    row_segment_ref,
    key_segment_ref,
    output_weight_ref,
    packed_ref,
    prob_out,
    rest_out,
    normed_out,
    send_ref,
    keep_ref,
    gathered,
    query,
    key,
    value,
    normed,
    prob,
    rest,
    weight,
    sems,
    normed_sem,
):
    head = pl.program_id(0)
    head_count = pl.num_programs(0)
    place = place_ref[0]
    for which, ref in enumerate((query_weight_ref, key_weight_ref, value_weight_ref)):
        weight[which * DH : which * DH + DH, :] = ref[...]
    blocks = (block0, block1, block2, block3)
    size = block0.shape[0]
    normed_copy = pltpu.make_async_copy(normed, normed_out, normed_sem)

    @pl.when(head == 0)
    def _():
        for step, block in enumerate(blocks):
            values = block[...].astype(F32)
            inverse = inverse_root(values)
            normed[step] = (values * inverse * gain_ref[...].astype(F32)).astype(BF)
        normed_copy.start()

    for step in range(4):
        row = pl.multiple_of((place ^ step) * size, size)
        rows = pl.ds(row, size)
        made = dot(normed[step], weight[...], ROWS_T).astype(BF)
        packed_ref[0, rows, : 3 * DH] = made
        query[rows, :] = made[:, :DH]
        key[rows, :] = made[:, DH : 2 * DH]
        value[rows, :] = made[:, 2 * DH :]
    key_segment = key_segment_ref[...].astype(F32)
    total = query.shape[0]
    left_bias = table_ref[15, head]
    right_bias = table_ref[31, head]
    spots = tiles_of(total)

    def copy_of(which, tile):
        return pltpu.make_async_copy(
            stored_tile(spots, which, tile, prob, rest),
            stored_tile(spots, which, tile, prob_out, rest_out),
            sems.at[which, tile],
        )

    for index, (row, first, keys, tile) in enumerate(spots):
        low, high, lane = pieces_of(tile, keys)
        rows = slice(row, row + QT)
        local = slice(tile * QT, tile * QT + QT)
        store = rest if first else prob
        scores = dot(query[rows, :], key[first : first + keys, :], ROWS_T)
        parts = []
        if low > 0:
            parts.append((0, low, scores[:, :low] + left_bias))
        parts.append((low, high, scores[:, low:high] + near_ref[0, :, lane : lane + high - low]))
        if high < keys:
            parts.append((high, keys, scores[:, high:] + right_bias))
        if first:
            row_segment = row_segment_ref[local, :1]
            parts = [
                (a, b, jnp.where(row_segment == key_segment[:, a:b], part, MASKED))
                for a, b, part in parts
            ]
        peak = functools.reduce(
            jnp.maximum, [jnp.max(part, axis=1, keepdims=True) for a, b, part in parts]
        )
        parts = [(a, b, jnp.exp(part - peak)) for a, b, part in parts]
        whole = sum(jnp.sum(part, axis=1, keepdims=True) for a, b, part in parts)
        share = 1.0 / whole
        for a, b, part in parts:
            store[head, local, a:b] = (part * share).astype(BF)
        made = dot(store[head, local, :], value[first : first + keys, :]).astype(BF)
        packed_ref[0, rows, 3 * DH :] = made
        copy_of(head, index).start()
    for which in range(gathered.shape[1] // DH):

        @pl.when(head == which)
        def _():
            gathered[:, which * DH : which * DH + DH] = packed_ref[0, :, 3 * DH :]

    @pl.when(head == head_count - 1)
    def _():
        for step in (1, 3, 2, 0):
            row = pl.multiple_of((place ^ step) * size, size)
            made = dot(gathered[pl.ds(row, size), :], output_weight_ref[...]).astype(BF)
            out = send_ref if step & 1 else keep_ref
            out[step >> 1] = made
        normed_copy.wait()
        for which in range(gathered.shape[1] // DH):
            for index in range(len(spots)):
                copy_of(which, index).wait()


def attend_forward(place, table, blocks, gain, weights, near, row_segment, key_segment, output_weight):
    size, width = blocks[0].shape
    head_count = near.shape[0]
    total = 4 * size
    rest = total - LONG
    by_head = lambda *shape: pl.BlockSpec((1, *shape), lambda h: (h, *(0 for _ in shape)))
    whole = lambda *shape: pl.BlockSpec(shape, lambda h: tuple(0 for _ in shape))
    apart = pl.BlockSpec(memory_space=pl.ANY)
    return pl.pallas_call(
        forward_kernel,
        grid=(head_count,),
        out_shape=(
            struct((head_count, total, 4 * DH), BF),
            struct((head_count, LONG, LONG), BF),
            struct((head_count, rest, rest), BF),
            struct((4, size, width), BF),
            struct((2, size, width), BF),
            struct((2, size, width), BF),
            struct((total, head_count * DH), BF),
        ),
        in_specs=[
            smem(),
            smem(),
            *(whole(size, width) for _ in range(4)),
            whole(1, width),
            *(pl.BlockSpec((DH, width), lambda h: (h, 0)) for _ in range(3)),
            by_head(QT, QT + 2 * NEAR),
            whole(rest, 128),
            whole(1, rest),
            whole(head_count * DH, width),
        ],
        out_specs=(
            by_head(total, 4 * DH),
            apart,
            apart,
            apart,
            whole(2, size, width),
            whole(2, size, width),
            whole(total, head_count * DH),
        ),
        scratch_shapes=[
            pltpu.VMEM((total, DH), BF),
            pltpu.VMEM((total, DH), BF),
            pltpu.VMEM((total, DH), BF),
            pltpu.VMEM((4, size, width), BF),
            pltpu.VMEM((head_count, LONG, LONG), BF),
            pltpu.VMEM((head_count, rest, rest), BF),
            pltpu.VMEM((3 * DH, width), BF),
            pltpu.SemaphoreType.DMA((head_count, total // QT)),
            pltpu.SemaphoreType.DMA,
        ],
        compiler_params=params(56),
        cost_estimate=LONG_KERNEL,
        name="attend_forward",
    )(place, table, *blocks, gain, *weights, near, row_segment, key_segment, output_weight)


def backward_kernel(
    place_ref,
    grad0,
    grad1,
    grad2,
    grad3,
    normed_in,
    output_weight_ref,
    packed_ref,
    gathered_ref,
    prob_in,
    rest_in,
    parts_ref,
    line_ref,
    kept_ref,
    away_ref,
    *more_refs,
):
    (
        normed,
        prob,
        rest,
        query,
        key,
        value,
        context,
        turned,
        context_grad,
        near_total,
        far_total,
        key_total,
        value_total,
        sums,
        sems,
        normed_sem,
    ) = more_refs
    head = pl.program_id(0)
    head_count = pl.num_programs(0)
    place = place_ref[0]
    bit = place_ref[1] & 1
    size = normed.shape[1]
    total = query.shape[0]
    spots = tiles_of(total)
    blocks = [pl.multiple_of((place ^ step) * size, size) for step in range(4)]
    normed_copy = pltpu.make_async_copy(normed_in, normed, normed_sem)

    def copy_of(which, tile):
        return pltpu.make_async_copy(
            stored_tile(spots, which, tile, prob_in, rest_in),
            stored_tile(spots, which, tile, prob, rest),
            sems.at[which, tile],
        )

    @pl.when(head == 0)
    def _():
        for which in range(prob.shape[0]):
            for index in range(len(spots)):
                copy_of(which, index).start()
            if which == 0:
                normed_copy.start()

    query[...] = packed_ref[0, :, :DH]
    key[...] = packed_ref[0, :, DH : 2 * DH]
    value[...] = packed_ref[0, :, 2 * DH : 3 * DH]
    context[...] = packed_ref[0, :, 3 * DH :]
    turned[...] = key[...].T
    whole = sums.shape[0] // 4

    @pl.when(head == 0)
    def _():
        output_grad = 0.0
        for row, grad in zip(blocks, (grad0, grad1, grad2, grad3)):
            rows = pl.ds(row, size)
            made = dot(grad[...], output_weight_ref[...], ROWS_T).astype(BF)
            for which in range(context_grad.shape[0]):
                context_grad[which, rows, :] = made[:, which * DH : which * DH + DH]
            output_grad += dot(gathered_ref[rows, :], grad[...], T_ROWS)
        sums[3 * whole :, :] = output_grad

    near_total[...] = jnp.zeros_like(near_total)
    far_total[...] = jnp.zeros_like(far_total)

    for index, (row, first, keys, tile) in enumerate(spots):
        low, high, lane = pieces_of(tile, keys)
        rows = slice(row, row + QT)
        span = slice(first, first + keys)
        local = slice(tile * QT, tile * QT + QT)
        grads = context_grad[head, rows, :]
        prob_grad = dot(grads, value[span, :], ROWS_T)
        row_dot = jnp.sum(
            grads.astype(F32) * context[rows, :].astype(F32), axis=1, keepdims=True
        )
        copy_of(head, index).wait()
        taken = (rest if first else prob)[head, local, :]
        score_grad = taken.astype(F32) * (prob_grad - row_dot)
        low_grad = score_grad.astype(BF)
        near_total[:, lane : lane + high - low] += score_grad[:, low:high]
        for side, (a, b) in enumerate(((0, low), (high, keys))):
            if b > a:
                far_total[side] += sum(score_grad[:, c : c + 128] for c in range(a, b, 128))
        parts_ref[0, :DH, rows] = dot(turned[:, span], low_grad, ROWS_T).astype(BF)
        value_part = dot(grads, taken, T_ROWS)
        key_part = dot(query[rows, :], low_grad, T_ROWS)
        if tile == 0:
            value_total[:, span] = value_part
            key_total[:, span] = key_part
        else:
            value_total[:, span] += value_part
            key_total[:, span] += key_part

    padded = jnp.concatenate(
        [near_total[...], jnp.zeros((QT, WIDE - near_total.shape[1]), F32)], axis=1
    )
    count = QT
    while count > 1:
        count //= 2
        padded = padded[:count] + pltpu.roll(padded[count:], WIDE - count, 1)
    line = pltpu.roll(padded, QT - 1, 1)
    lanes = lax.broadcasted_iota(jnp.int32, line.shape, 1)
    line = jnp.where(lanes == 0, jnp.sum(far_total[0]), line)
    line_ref[0] = jnp.where(lanes == WIDE - 1, jnp.sum(far_total[1]), line)

    parts_ref[0, DH : 2 * DH, :] = key_total[...].astype(BF)
    parts_ref[0, 2 * DH :, :] = value_total[...].astype(BF)

    @pl.when(head == 0)
    def _():
        normed_copy.wait()

    made = sum(
        dot(parts_ref[0, :, pl.ds(row, size)], normed[step])
        for step, row in enumerate(blocks)
    )
    for which in range(3):
        row = pl.multiple_of(which * whole + head * DH, DH)
        sums[pl.ds(row, DH), :] = made[which * DH : which * DH + DH]

    @pl.when(head == head_count - 1)
    def _():
        half = kept_ref.shape[0]
        for flip, out in enumerate((kept_ref, away_ref)):
            row = pl.multiple_of((bit ^ flip) * half, half)
            out[...] = sums[pl.ds(row, half), :].astype(out.dtype)


def attend_backward(place, grads, normed, output_weights, kept):
    packed, prob, rest, gathered = kept
    _, size, width = normed.shape
    head_count, total, _ = packed.shape
    rows = 4 * DH * head_count
    by_head = lambda *shape: pl.BlockSpec((1, *shape), lambda h: (h, *(0 for _ in shape)))
    whole = lambda *shape: pl.BlockSpec(shape, lambda h: tuple(0 for _ in shape))
    apart = pl.BlockSpec(memory_space=pl.ANY)
    return pl.pallas_call(
        backward_kernel,
        grid=(head_count,),
        out_shape=(
            struct((head_count, 3 * DH, total), BF),
            struct((head_count, 1, WIDE), F32),
            struct((rows // 2, width), F32),
            struct((rows // 2, width), BF),
        ),
        in_specs=[
            smem(),
            *(whole(size, width) for _ in range(4)),
            apart,
            whole(head_count * DH, width),
            by_head(total, 4 * DH),
            whole(total, head_count * DH),
            apart,
            apart,
        ],
        out_specs=(
            by_head(3 * DH, total),
            by_head(1, WIDE),
            whole(rows // 2, width),
            whole(rows // 2, width),
        ),
        scratch_shapes=[
            pltpu.VMEM(normed.shape, BF),
            pltpu.VMEM(prob.shape, BF),
            pltpu.VMEM(rest.shape, BF),
            *(pltpu.VMEM((total, DH), BF) for _ in range(4)),
            pltpu.VMEM((DH, total), BF),
            pltpu.VMEM((head_count, total, DH), BF),
            pltpu.VMEM((QT, QT + 2 * NEAR), F32),
            pltpu.VMEM((2, QT, 128), F32),
            pltpu.VMEM((DH, total), F32),
            pltpu.VMEM((DH, total), F32),
            pltpu.VMEM((rows, width), F32),
            pltpu.SemaphoreType.DMA((head_count, total // QT)),
            pltpu.SemaphoreType.DMA,
        ],
        compiler_params=params(56),
        cost_estimate=LONG_KERNEL,
        name="attend_backward",
    )(place, *grads, normed, output_weights, packed, gathered, prob, rest)


def normed_grad_kernel(
    place_ref,
    parts_ref,
    query_weight_ref,
    key_weight_ref,
    value_weight_ref,
    gain_ref,
    normed_ref,
    gain_two_ref,
    line_ref,
    away_ref,
    send_ref,
    keep_ref,
    rider_ref,
    loaded_ref,
):
    place = place_ref[0]
    size = normed_ref.shape[1]
    gain_grad = 0.0
    weights = (query_weight_ref, key_weight_ref, value_weight_ref)
    for step in range(4):
        row = pl.multiple_of((place ^ step) * size, size)
        made = 0.0
        for head in range(parts_ref.shape[0]):
            weight = jnp.concatenate([ref[head * DH : head * DH + DH, :] for ref in weights])
            made += dot(parts_ref[head, :, pl.ds(row, size)], weight, T_ROWS)
        out = send_ref if step & 1 else keep_ref
        out[step >> 1] = made.astype(BF)
        gain_grad += jnp.sum(made * normed_ref[step].astype(F32), axis=0, keepdims=True)
    rider_ref[...] = jnp.zeros_like(rider_ref)
    rider_ref[0:1, :] = gain_grad / gain_ref[...].astype(F32)
    rider_ref[1:2, :] = gain_two_ref[...]
    for head in range(line_ref.shape[0]):
        rider_ref[2 + head : 3 + head, :] = line_ref[head]
    half = away_ref.shape[0]
    loaded_ref[:half, :] = away_ref[...]
    loaded_ref[half:, :] = rider_ref[...].astype(BF)


def normed_grad(place, parts, weights, gain, normed, gain_two_grad, lines, away):
    _, size, width = normed.shape
    operands = (parts, *weights, gain, normed, gain_two_grad, lines, away)
    return call(
        normed_grad_kernel,
        "normed_grad",
        (
            struct((2, size, width), BF),
            struct((2, size, width), BF),
            struct((RIDER, width), F32),
            struct((away.shape[0] + RIDER, width), BF),
        ),
        (smem(), *operands),
        (place, *operands),
        cost=LONG_KERNEL,
    )


def inverse_root(values):
    return lax.rsqrt(jnp.mean(values * values, axis=-1, keepdims=True) + EPSILON)


def norm_input_grad(values, inverse, gains, upstream):
    scaled = upstream * gains
    projection = jnp.mean(scaled * values, axis=-1, keepdims=True)
    return inverse * scaled - values * (inverse * inverse * inverse) * projection


def middle_grad_kernel(
    cotangent_ref, middle_ref, own_ref, near_ref, far_ref, gain_ref, grad_ref, low_ref, gain_grad_ref
):
    upstream = own_ref[...].astype(F32) + near_ref[...].astype(F32) + far_ref[...].astype(F32)
    values = middle_ref[...]
    inverse = inverse_root(values)
    grad = cotangent_ref[...].astype(F32) + norm_input_grad(
        values, inverse, gain_ref[...].astype(F32), upstream
    )
    grad_ref[...] = grad
    low_ref[...] = grad.astype(BF)
    gain_grad_ref[...] = jnp.sum(upstream * values * inverse, axis=0, keepdims=True)


def make_middle_grad(cotangent, middle, sums, gain):
    shape = middle.shape
    operands = (cotangent, middle, *sums, gain)
    return call(
        middle_grad_kernel,
        "middle_grad",
        (struct(shape, F32), struct(shape, BF), struct((1, shape[1]), F32)),
        operands,
        operands,
    )


def input_grad_kernel(input_ref, own_ref, near_ref, far_ref, gain_ref, middle_ref, out_ref):
    upstream = own_ref[0].astype(F32) + near_ref[0].astype(F32) + far_ref[...].astype(F32)
    values = input_ref[...].astype(F32)
    out_ref[...] = middle_ref[...] + norm_input_grad(
        values, inverse_root(values), gain_ref[...], upstream
    )


def make_input_grad(inputs, sums, gain, middle_grad):
    first = one((1, *inputs.shape))
    return call(
        input_grad_kernel,
        "input_grad",
        (struct(inputs.shape, F32),),
        (inputs, first, first, sums[2], gain, middle_grad),
        (inputs, *sums, gain, middle_grad),
    )[0]


def layer_output_kernel(middle_ref, own_ref, near_ref, far_ref, out_ref):
    own, near, far = (ref[...].astype(F32) for ref in (own_ref, near_ref, far_ref))
    out_ref[...] = (middle_ref[...] + (own + near + far)).astype(BF)


def make_layer_output(middle, sums):
    operands = (middle, *sums)
    return call(
        layer_output_kernel, "layer_output", (struct(middle.shape, BF),), operands, operands
    )[0]


def outer_kernel(weight_ref, *refs):
    hidden_refs, out_refs = refs[:4], refs[4:]
    for hidden, out in zip(hidden_refs, out_refs):
        out[...] = dot(hidden[...], weight_ref[...]).astype(BF)


def outer_product(hidden, weight):
    operands = (weight, *hidden)
    shape = struct((hidden[0].shape[0], weight.shape[1]), BF)
    return call(outer_kernel, "outer", (shape,) * 4, operands, operands, cost=LONG_KERNEL)


def after(values, *others):
    return lax.optimization_barrier((values, others))[0]


def across(values, axis, flip):
    count = lax.axis_size(axis)
    return lax.ppermute(values, axis, [(i, i ^ flip) for i in range(count)])


def over_core(values):
    return across(values, "tensor", 1)


def over_x(values):
    return across(values, "tensor", 2)


def usual():
    return lax.axis_size("dp") == 8


def split_kernel(place_ref, *refs):
    kept_ref, came_ref, *refs = refs
    riders, refs = refs[:-4], refs[-4:]
    own_ref, *away_refs = refs
    size = own_ref.shape[0]
    spot = place_ref[1] >> 1
    if riders:
        rider_ref, total_ref = riders
        half = kept_ref.shape[0]
        total_ref[...] = rider_ref[...] + came_ref[half:, :].astype(F32)
        for out in away_refs:
            out[size:, :] = total_ref[...].astype(BF)
    for flip, out in enumerate((own_ref, *away_refs)):
        rows = pl.ds(pl.multiple_of((spot ^ flip) * size, size), size)
        out[:size, :] = (kept_ref[rows, :] + came_ref[rows, :].astype(F32)).astype(out.dtype)


def four_kernel(own_ref, came0, came1, came2, *refs):
    *riders, out_ref = refs
    size = own_ref.shape[0]
    total = own_ref[...]
    for came in (came0, came1, came2):
        total += came[:size, :].astype(F32)
    out_ref[...] = total.astype(BF)
    if riders:
        rider_ref, sum_ref = riders
        total = rider_ref[...]
        for came in (came0, came1, came2):
            total += came[size:, :].astype(F32)
        sum_ref[...] = total


def pair_kernel(place_ref, own_ref, came_ref, out_ref):
    size = own_ref.shape[0]
    bit = (place_ref[1] >> 2) & 1
    for flip, ref in enumerate((own_ref, came_ref)):
        out_ref[pl.ds(pl.multiple_of((bit ^ flip) * size, size), size), :] = ref[...]


def half_kernel(place_ref, pair_ref, came_ref, out_ref):
    size = pair_ref.shape[0] // 2
    bit = (place_ref[1] >> 1) & 1
    for flip, ref in enumerate((pair_ref, came_ref)):
        for which in range(2):
            row = pl.multiple_of(((bit ^ flip) + 2 * which) * size, size)
            out_ref[pl.ds(row, size), :] = ref[which * size : which * size + size, :]


def join_kernel(place_ref, own_ref, came0, came1, came2, out_ref):
    size = own_ref.shape[0]
    spot = place_ref[1] >> 1
    for flip, ref in enumerate((own_ref, came0, came1, came2)):
        out_ref[pl.ds(pl.multiple_of((spot ^ flip) * size, size), size), :] = ref[...]


def whole_kernel(factor, pieces, place_ref, own_ref, came_ref, *refs):
    *out_refs, whole = refs
    part = own_ref.shape[0] // pieces
    bit = place_ref[1] & 1
    for flip, ref in enumerate((own_ref, came_ref)):
        for piece in range(pieces):
            row = pl.multiple_of((2 * piece + (bit ^ flip)) * part, part)
            whole[pl.ds(row, part), :] = ref[piece * part : piece * part + part, :]
    rows = whole.shape[0] // len(out_refs)
    for index, out in enumerate(out_refs):
        out[...] = whole[index * rows : index * rows + rows, :].astype(F32) * factor


def cut_kernel(place_ref, *refs):
    whole_refs, kept_ref, away_ref = refs[:-2], refs[-2], refs[-1]
    bit = place_ref[1] & 1
    half = whole_refs[0].shape[0] // 2
    for index, ref in enumerate(whole_refs):
        here = slice(index * half, index * half + half)
        for flip, out in enumerate((kept_ref, away_ref)):
            rows = pl.ds(pl.multiple_of((bit ^ flip) * half, half), half)
            out[here, :] = ref[rows, :].astype(out.dtype)


def cut(place, arrays):
    rows, width = arrays[0].shape
    shape = (len(arrays) * rows // 2, width)
    return call(
        cut_kernel, "cut", (struct(shape, F32), struct(shape, BF)), (smem(), *arrays), (place, *arrays)
    )


class Reduction:
    def __init__(self, name, place, pieces, kept, away, rider=None):
        self.name, self.place, self.pieces, self.rider = name, place, pieces, rider
        self.rows, self.width = 2 * kept.shape[0], kept.shape[1]
        self.stage = 0
        self.count = lax.axis_size("dp")
        self.halves = (kept, away[: kept.shape[0]])
        self.kept = kept
        if self.count == 8:
            self.came = across(away, "dp", 1)

    def step(self, *others):
        self.stage += 1
        if self.count != 8:
            if self.stage == 1 and self.rider is not None:
                self.rider = lax.psum(self.rider, "dp")
            return self.kept
        width = self.width
        name = f"{self.name}_{self.stage}"
        riders = () if self.rider is None else (self.rider,)
        also = tuple(struct(item.shape, F32) for item in riders)
        if self.stage == 1:
            size = self.rows // 8
            far = size + sum(item.shape[0] for item in riders)
            operands = (self.kept, after(self.came, *others), *riders)
            *riders, own, a, b, c = call(
                split_kernel,
                name,
                (*also, struct((size, width), F32), *(struct((far, width), BF) for _ in range(3))),
                (smem(), *operands),
                (self.place, *operands),
                cost=FREE if self.rider is None else LONG_KERNEL,
            )
            self.kept = own
            self.came = [across(item, "dp", 2 * flip) for flip, item in enumerate((a, b, c), 1)]
            self.rider = riders[0] if riders else None
            return own
        if self.stage == 2:
            operands = (self.kept, *after(self.came, *others), *riders)
            *riders, low = call(
                four_kernel, name, (*also, struct(self.kept.shape, BF)), operands, operands
            )
            self.kept = low
            if riders:
                self.came = [across(low, "dp", 2 * flip) for flip in range(1, 4)]
                self.rider = riders[0]
            else:
                self.came = across(low, "dp", 4)
            return low
        if self.rider is None:
            flip, kernel = {3: (2, pair_kernel), 4: (1, half_kernel)}[self.stage]
            operands = (self.kept, after(self.came, *others))
            rows = 2 * self.kept.shape[0]
            self.kept = call(
                kernel,
                name,
                (struct((rows, width), BF),),
                (smem(), *operands),
                (self.place, *operands),
                cost=LONG_KERNEL if self.stage == 3 else FREE,
            )[0]
            self.came = across(self.kept, "dp", flip)
            return self.kept
        if self.stage == 3:
            operands = (self.kept, *after(self.came, *others))
            half = call(
                join_kernel,
                name,
                (struct((self.rows // 2, width), BF),),
                (smem(), *operands),
                (self.place, *operands),
            )[0]
            self.kept = half
            self.came = across(half, "dp", 1)
            return half
        raise ValueError("over")

    def finish(self, factor, count, *others):
        own, came = self.kept, self.came if self.count == 8 else None
        if self.count != 8:
            kept, away = self.halves
            bit = lax.axis_index("dp") & 1
            away = away.astype(F32)
            first = jnp.where(bit == 0, kept, away)
            second = jnp.where(bit == 0, away, kept)
            total = sum_over_dp(jnp.concatenate([first, second])).astype(BF)
            half = kept.shape[0]
            own = lax.dynamic_slice_in_dim(total, bit * half, half)
            came = lax.dynamic_slice_in_dim(total, (1 - bit) * half, half)
        operands = (own, after(came, *others))
        width = self.width
        return call(
            functools.partial(whole_kernel, factor, self.pieces),
            self.name,
            (struct((self.rows // count, width), F32),) * count,
            (smem(), *operands),
            (self.place, *operands),
            (pltpu.VMEM((self.rows, width), BF),),
        )


def sum_over_dp(values):
    count = lax.axis_size("dp")
    if count & (count - 1) or values.shape[0] % count:
        return lax.psum(values, "dp")
    index = lax.axis_index("dp")
    bits = count.bit_length() - 1
    for bit in range(bits):
        half = values.shape[0] // 2
        mine = (index >> bit) & 1
        keep = lax.dynamic_slice_in_dim(values, mine * half, half)
        away = lax.dynamic_slice_in_dim(values, (1 - mine) * half, half)
        values = keep + across(away.astype(BF), "dp", 1 << bit).astype(F32)
    values = values.astype(BF)
    for bit in reversed(range(bits)):
        mine = (index >> bit) & 1
        came = across(values, "dp", 1 << bit)
        first = jnp.where(mine == 0, values, came)
        second = jnp.where(mine == 0, came, values)
        values = jnp.concatenate([first, second])
    return values.astype(F32)


ROOT = 0.7978845608028654
CUBE = 0.044715


def gate(value):
    square = value * value
    tanh = jnp.tanh(ROOT * value * (1.0 + CUBE * square))
    half = 0.5 * (1.0 + tanh)
    slope = half + 0.5 * ROOT * value * (1.0 - tanh * tanh) * (1.0 + 3.0 * CUBE * square)
    return value * half, slope


def body(
    inputs,
    segments,
    first_gain,
    query_weight,
    lookup_projection,
    value_weight,
    output_weight,
    bucket_bias_table,
    second_gain,
    inner_weight,
    outer_weight,
    cotangent,
):
    total = segments.shape[0]
    size, width = inputs.shape
    head_count = query_weight.shape[1] // DH
    factor = float(total * lax.axis_size("dp")) ** (-0.5)

    far, near_block = over_x(inputs), over_core(inputs)
    place = jnp.stack([lax.axis_index("tensor"), lax.axis_index("dp")]).astype(jnp.int32)
    gain_one = first_gain.astype(F32)
    gain_two = second_gain.astype(F32)
    gain_row = gain_one.reshape(1, -1)
    table = bucket_bias_table.astype(F32)
    weights = (query_weight.T, lookup_projection.T, value_weight.T)
    key_segment = segments[LONG:].reshape(1, -1)
    near, row_segment = near_bias(table, key_segment)
    norm_input = inputs.astype(F32)
    inverse_one = inverse_root(norm_input)
    far = after(far, near, row_segment, place, gain_row, inverse_one)
    blocks = (inputs, near_block, far, over_core(far))
    cot_far = over_x(after(cotangent, far))
    cot_near = over_core(after(cotangent, far))

    *kept, normed_one, send, keep, gathered = attend_forward(
        place, table, blocks, gain_row, weights, near, row_segment, key_segment, output_weight
    )
    kept.append(gathered)
    cot_far = after(cot_far, keep)
    send = after(send, cot_far)
    near_sums = [None, over_core(send[1])]
    near_sums[0] = over_core(after(send[0], near_sums[1]))
    outward = (keep[1].astype(F32) + near_sums[1].astype(F32)).astype(BF)
    far_sum = over_x(outward)
    cot_far = after(cot_far, outward)
    cotangents = (cotangent, cot_near, cot_far, over_core(cot_far))
    hidden_grads = {}
    for step in (2, 3):
        hidden_grads[step] = dot(cotangents[step], outer_weight, ROWS_T)
    far_sum = after(far_sum, hidden_grads)

    middle = norm_input + (
        keep[0].astype(F32) + near_sums[0].astype(F32) + far_sum.astype(F32)
    )
    inverse_two = inverse_root(middle)
    low = (middle * inverse_two * gain_two).astype(BF)
    normed_two = [low, over_core(low), over_x(low)]

    hidden, inner_grads, second = {}, {}, {}

    def feed(step):
        values, slope = gate(dot(normed_two[step], inner_weight))
        hidden[step] = values.astype(BF)
        if step not in hidden_grads:
            hidden_grads[step] = dot(cotangents[step], outer_weight, ROWS_T)
        inner_grads[step] = (hidden_grads[step] * slope).astype(BF)
        second[step] = dot(inner_grads[step], inner_weight, ROWS_T).astype(BF)

    def weight_grads(steps):
        outer = sum(dot(hidden[step], cotangents[step], T_ROWS) for step in steps)
        inner = sum(dot(normed_two[step], inner_grads[step], T_ROWS) for step in steps)
        return outer, inner

    feed(0)
    feed(1)
    second_near_one = over_core(second[1])
    first_grads = weight_grads((0, 1))
    normed_two[2] = after(normed_two[2], second, first_grads)
    normed_two.append(over_core(normed_two[2]))
    feed(2)
    normed_two[3] = after(normed_two[3], second[2])
    feed(3)
    second_near_three = over_core(second[3])
    outward = (second[2].astype(F32) + second_near_three.astype(F32)).astype(BF)
    second_far = over_x(outward)

    far_grads = after((hidden[2], hidden[3], inner_grads[2], inner_grads[3]), outward)
    hidden[2], hidden[3], inner_grads[2], inner_grads[3] = far_grads
    outer_grad, inner_grad = (
        left + right for left, right in zip(first_grads, weight_grads((2, 3)))
    )
    feed_sum = Reduction("feed_sum", place, 2, *cut(place, (outer_grad, inner_grad)))

    second_far = after(second_far, feed_sum.kept)
    middle_grad, low, gain_two_grad = make_middle_grad(
        cotangent, middle, (second[0], second_near_one, second_far), gain_two.reshape(1, -1)
    )
    grads = [low, over_core(low), over_x(low)]
    outer_parts = outer_product(after([hidden[step] for step in range(4)], low), outer_weight)
    outer_near = [over_core(outer_parts[1]), over_core(outer_parts[3])]
    grads[2] = after(grads[2], outer_parts)
    grads.append(over_core(grads[2]))
    mark = feed_sum.step(grads[3])

    parts, lines, held, away = attend_backward(
        place, after(grads, mark), normed_one, output_weight, kept
    )
    outward = after(outer_parts[2], held).astype(F32) + outer_near[1].astype(F32)
    outward = outward.astype(BF)
    outer_far = over_x(outward)
    mark = feed_sum.step(held)
    send, keep, rider, loaded = normed_grad(
        place, after(parts, mark), weights, gain_row, normed_one, gain_two_grad, lines, away
    )
    attention_sum = Reduction("attention_sum", place, 1, held, loaded, rider)
    layer_output = make_layer_output(
        middle, (outer_parts[0], outer_near[0], after(outer_far, keep))
    )
    first_near = over_core(send)
    mark = feed_sum.step(layer_output)
    mark = attention_sum.step(mark)
    outward = keep[1].astype(F32) + after(first_near[1], mark).astype(F32)
    outward = outward.astype(BF)
    first_far = over_x(outward)
    mark = feed_sum.step(outward)
    input_grad = make_input_grad(
        inputs, (keep, first_near, after(first_far, mark)), gain_row, middle_grad
    )
    mark = attention_sum.step(input_grad)
    small = attention_sum.rider
    gains = small[:8] + over_core(small[:8])
    mark = attention_sum.step(mark)
    outer_weight_grad, inner_weight_grad = feed_sum.finish(factor, 2, mark)
    gain_grads = (gains + over_x(gains))[:2]
    query_grad, key_grad, value_grad, output_weight_grad = attention_sum.finish(
        factor, 4, inner_weight_grad
    )

    slots = jnp.arange(table.shape[0], dtype=jnp.int32)
    offsets = jnp.arange(WIDE, dtype=jnp.int32) - (QT + NEAR - 1)
    chosen = buckets_of(offsets)[None, :] == slots[:, None]
    table_grad = jnp.sum(
        jnp.where(chosen[:, None, :], small[2 : 2 + head_count][None], 0.0), axis=2
    )
    return (
        layer_output,
        input_grad,
        query_grad.T,
        key_grad.T,
        value_grad.T,
        output_weight_grad,
        table_grad * factor,
        inner_weight_grad,
        outer_weight_grad,
        gain_grads * factor,
    )


def solution(mesh):
    return jax.shard_map(
        body,
        mesh=mesh,
        in_specs=(
            P(("dp", "tensor"), None),
            P("dp"),
            P(),
            P(None, "tensor"),
            P(None, "tensor"),
            P(None, "tensor"),
            P("tensor", None),
            P(None, "tensor"),
            P(),
            P(None, "tensor"),
            P("tensor", None),
            P(("dp", "tensor"), None),
        ),
        out_specs=(
            P(("dp", "tensor"), None),
            P(("dp", "tensor"), None),
            P(None, "tensor"),
            P(None, "tensor"),
            P(None, "tensor"),
            P("tensor", None),
            P(None, "tensor"),
            P(None, "tensor"),
            P("tensor", None),
            P(),
        ),
        check_vma=False,
    )
```

```python
import functools

import jax
import jax.numpy as jnp
from jax import lax
from jax.experimental import pallas as pl
from jax.experimental.pallas import tpu as pltpu
from jax.sharding import PartitionSpec as P

DH = 64
LONG = 1024
QT = 256
NEAR = 128
WIDE = 768
RIDER = 16
EDGES = (8, 12, 16, 23, 32, 46, 64, 91)
EPSILON = 1e-06
MASKED = -1000000000.0
BF = jnp.bfloat16
F32 = jnp.float32


def buckets_of(offset):
    distance = jnp.abs(offset)
    coarse = jnp.full(distance.shape, 7, jnp.int32)
    for boundary in EDGES:
        coarse = coarse + (distance >= boundary).astype(jnp.int32)
    bucket = jnp.where(distance < 8, distance, coarse)
    return bucket + jnp.where(offset > 0, 16, 0).astype(jnp.int32)


def dot(left, right, dims=((1,), (0,))):
    return lax.dot_general(left, right, (dims, ((), ())), preferred_element_type=F32)


ROWS_T = ((1,), (1,))
T_ROWS = ((0,), (0,))


FREE = pl.CostEstimate(flops=0, bytes_accessed=0, transcendentals=0)
LONG_KERNEL = pl.CostEstimate(flops=200_000_000_000, bytes_accessed=0, transcendentals=0)


def params(limit=30):
    return pltpu.CompilerParams(vmem_limit_bytes=limit * 1024 * 1024)


def struct(shape, dtype):
    return jax.ShapeDtypeStruct(shape, dtype)


def one(shape, *index):
    index = index + (0,) * (len(shape) - len(index))
    return pl.BlockSpec(shape, lambda i: index)


def call(kernel, name, outs, ins, operands, scratch=(), cost=FREE):
    spec = lambda item: item if isinstance(item, pl.BlockSpec) else one(item.shape)
    return pl.pallas_call(
        kernel,
        grid=(1,),
        out_shape=outs,
        in_specs=[spec(item) for item in ins],
        out_specs=tuple(one(o.shape) for o in outs),
        scratch_shapes=scratch,
        compiler_params=params(),
        cost_estimate=cost,
        name=name,
    )(*operands)


def vmem():
    return pl.BlockSpec(memory_space=pltpu.VMEM)


def smem():
    return pl.BlockSpec(memory_space=pltpu.SMEM)


def near_kernel(table_ref, segment_ref, near_ref, column_ref):
    head_count = near_ref.shape[0]
    line = segment_ref[...].astype(F32)
    column_ref[...] = jnp.broadcast_to(line, (column_ref.shape[1], line.shape[1])).T
    lane = lax.broadcasted_iota(jnp.int32, (8, WIDE), 1)
    bucket = buckets_of(lane - (QT + NEAR - 1))
    for head in range(head_count):
        line = jnp.zeros((8, WIDE), F32)
        for slot in range(table_ref.shape[0]):
            line = jnp.where(bucket == slot, table_ref[slot, head], line)
        rows = jnp.broadcast_to(line[:1], (QT, WIDE))
        turned = pltpu.roll(rows, WIDE - QT + 1, 1, stride=1, stride_axis=0)
        near_ref[head] = turned[:, : QT + 2 * NEAR]


def near_bias(table, segments):
    head_count = table.shape[1]
    return pl.pallas_call(
        near_kernel,
        out_shape=(
            struct((head_count, QT, QT + 2 * NEAR), F32),
            struct((segments.shape[1], 128), F32),
        ),
        in_specs=[smem(), vmem()],
        out_specs=(vmem(), vmem()),
        compiler_params=params(),
        name="near_bias",
    )(table, segments)


def pieces_of(tile, keys):
    low = max(tile * QT - NEAR, 0)
    high = min(tile * QT + QT + NEAR, keys)
    return low, high, low - (tile * QT - NEAR)


def tiles_of(total):
    ranges = [(0, LONG)] + ([(LONG, total - LONG)] if total > LONG else [])
    return [
        (first + tile * QT, first, keys, tile)
        for first, keys in ranges
        for tile in range(keys // QT)
    ]


def stored_tile(spots, head, tile, prob, rest):
    row, first, keys, number = spots[tile]
    return (rest if first else prob).at[head, pl.ds(number * QT, QT), :]


def forward_kernel(
    place_ref,
    table_ref,
    block0,
    block1,
    block2,
    block3,
    gain_ref,
    query_weight_ref,
    key_weight_ref,
    value_weight_ref,
    near_ref,
    row_segment_ref,
    key_segment_ref,
    output_weight_ref,
    packed_ref,
    prob_out,
    rest_out,
    normed_out,
    send_ref,
    keep_ref,
    gathered,
    query,
    key,
    value,
    normed,
    prob,
    rest,
    weight,
    sems,
    normed_sem,
):
    head = pl.program_id(0)
    head_count = pl.num_programs(0)
    place = place_ref[0]
    for which, ref in enumerate((query_weight_ref, key_weight_ref, value_weight_ref)):
        weight[which * DH : which * DH + DH, :] = ref[...]
    blocks = (block0, block1, block2, block3)
    size = block0.shape[0]
    normed_copy = pltpu.make_async_copy(normed, normed_out, normed_sem)

    @pl.when(head == 0)
    def _():
        for step, block in enumerate(blocks):
            values = block[...].astype(F32)
            inverse = inverse_root(values)
            normed[step] = (values * inverse * gain_ref[...].astype(F32)).astype(BF)
        normed_copy.start()

    for step in range(4):
        row = pl.multiple_of((place ^ step) * size, size)
        rows = pl.ds(row, size)
        made = dot(normed[step], weight[...], ROWS_T).astype(BF)
        packed_ref[0, rows, : 3 * DH] = made
        query[rows, :] = made[:, :DH]
        key[rows, :] = made[:, DH : 2 * DH]
        value[rows, :] = made[:, 2 * DH :]
    key_segment = key_segment_ref[...].astype(F32)
    total = query.shape[0]
    left_bias = table_ref[15, head]
    right_bias = table_ref[31, head]
    spots = tiles_of(total)

    def copy_of(which, tile):
        return pltpu.make_async_copy(
            stored_tile(spots, which, tile, prob, rest),
            stored_tile(spots, which, tile, prob_out, rest_out),
            sems.at[which, tile],
        )

    for index, (row, first, keys, tile) in enumerate(spots):
        low, high, lane = pieces_of(tile, keys)
        rows = slice(row, row + QT)
        local = slice(tile * QT, tile * QT + QT)
        store = rest if first else prob
        scores = dot(query[rows, :], key[first : first + keys, :], ROWS_T)
        parts = []
        if low > 0:
            parts.append((0, low, scores[:, :low] + left_bias))
        parts.append((low, high, scores[:, low:high] + near_ref[0, :, lane : lane + high - low]))
        if high < keys:
            parts.append((high, keys, scores[:, high:] + right_bias))
        if first:
            row_segment = row_segment_ref[local, :1]
            parts = [
                (a, b, jnp.where(row_segment == key_segment[:, a:b], part, MASKED))
                for a, b, part in parts
            ]
        peak = functools.reduce(
            jnp.maximum, [jnp.max(part, axis=1, keepdims=True) for a, b, part in parts]
        )
        parts = [(a, b, jnp.exp(part - peak)) for a, b, part in parts]
        whole = sum(jnp.sum(part, axis=1, keepdims=True) for a, b, part in parts)
        share = 1.0 / whole
        for a, b, part in parts:
            store[head, local, a:b] = (part * share).astype(BF)
        made = dot(store[head, local, :], value[first : first + keys, :]).astype(BF)
        packed_ref[0, rows, 3 * DH :] = made
        copy_of(head, index).start()
    for which in range(gathered.shape[1] // DH):

        @pl.when(head == which)
        def _():
            gathered[:, which * DH : which * DH + DH] = packed_ref[0, :, 3 * DH :]

    @pl.when(head == head_count - 1)
    def _():
        for step in (1, 3, 2, 0):
            row = pl.multiple_of((place ^ step) * size, size)
            made = dot(gathered[pl.ds(row, size), :], output_weight_ref[...]).astype(BF)
            out = send_ref if step & 1 else keep_ref
            out[step >> 1] = made
        normed_copy.wait()
        for which in range(gathered.shape[1] // DH):
            for index in range(len(spots)):
                copy_of(which, index).wait()


def attend_forward(place, table, blocks, gain, weights, near, row_segment, key_segment, output_weight):
    size, width = blocks[0].shape
    head_count = near.shape[0]
    total = 4 * size
    rest = total - LONG
    by_head = lambda *shape: pl.BlockSpec((1, *shape), lambda h: (h, *(0 for _ in shape)))
    whole = lambda *shape: pl.BlockSpec(shape, lambda h: tuple(0 for _ in shape))
    apart = pl.BlockSpec(memory_space=pl.ANY)
    return pl.pallas_call(
        forward_kernel,
        grid=(head_count,),
        out_shape=(
            struct((head_count, total, 4 * DH), BF),
            struct((head_count, LONG, LONG), BF),
            struct((head_count, rest, rest), BF),
            struct((4, size, width), BF),
            struct((2, size, width), BF),
            struct((2, size, width), BF),
            struct((total, head_count * DH), BF),
        ),
        in_specs=[
            smem(),
            smem(),
            *(whole(size, width) for _ in range(4)),
            whole(1, width),
            *(pl.BlockSpec((DH, width), lambda h: (h, 0)) for _ in range(3)),
            by_head(QT, QT + 2 * NEAR),
            whole(rest, 128),
            whole(1, rest),
            whole(head_count * DH, width),
        ],
        out_specs=(
            by_head(total, 4 * DH),
            apart,
            apart,
            apart,
            whole(2, size, width),
            whole(2, size, width),
            whole(total, head_count * DH),
        ),
        scratch_shapes=[
            pltpu.VMEM((total, DH), BF),
            pltpu.VMEM((total, DH), BF),
            pltpu.VMEM((total, DH), BF),
            pltpu.VMEM((4, size, width), BF),
            pltpu.VMEM((head_count, LONG, LONG), BF),
            pltpu.VMEM((head_count, rest, rest), BF),
            pltpu.VMEM((3 * DH, width), BF),
            pltpu.SemaphoreType.DMA((head_count, total // QT)),
            pltpu.SemaphoreType.DMA,
        ],
        compiler_params=params(56),
        cost_estimate=LONG_KERNEL,
        name="attend_forward",
    )(place, table, *blocks, gain, *weights, near, row_segment, key_segment, output_weight)


def backward_kernel(
    place_ref,
    grad0,
    grad1,
    grad2,
    grad3,
    normed_in,
    output_weight_ref,
    packed_ref,
    gathered_ref,
    prob_in,
    rest_in,
    parts_ref,
    line_ref,
    kept_ref,
    away_ref,
    *more_refs,
):
    (
        normed,
        prob,
        rest,
        query,
        key,
        value,
        context,
        turned,
        context_grad,
        near_total,
        far_total,
        key_total,
        value_total,
        sums,
        sems,
        normed_sem,
    ) = more_refs
    head = pl.program_id(0)
    head_count = pl.num_programs(0)
    place = place_ref[0]
    bit = place_ref[1] & 1
    size = normed.shape[1]
    total = query.shape[0]
    spots = tiles_of(total)
    blocks = [pl.multiple_of((place ^ step) * size, size) for step in range(4)]
    normed_copy = pltpu.make_async_copy(normed_in, normed, normed_sem)

    def copy_of(which, tile):
        return pltpu.make_async_copy(
            stored_tile(spots, which, tile, prob_in, rest_in),
            stored_tile(spots, which, tile, prob, rest),
            sems.at[which, tile],
        )

    @pl.when(head == 0)
    def _():
        for which in range(prob.shape[0]):
            for index in range(len(spots)):
                copy_of(which, index).start()
            if which == 0:
                normed_copy.start()

    query[...] = packed_ref[0, :, :DH]
    key[...] = packed_ref[0, :, DH : 2 * DH]
    value[...] = packed_ref[0, :, 2 * DH : 3 * DH]
    context[...] = packed_ref[0, :, 3 * DH :]
    turned[...] = key[...].T
    whole = sums.shape[0] // 4

    @pl.when(head == 0)
    def _():
        output_grad = 0.0
        for row, grad in zip(blocks, (grad0, grad1, grad2, grad3)):
            rows = pl.ds(row, size)
            made = dot(grad[...], output_weight_ref[...], ROWS_T).astype(BF)
            for which in range(context_grad.shape[0]):
                context_grad[which, rows, :] = made[:, which * DH : which * DH + DH]
            output_grad += dot(gathered_ref[rows, :], grad[...], T_ROWS)
        sums[3 * whole :, :] = output_grad

    near_total[...] = jnp.zeros_like(near_total)
    far_total[...] = jnp.zeros_like(far_total)

    for index, (row, first, keys, tile) in enumerate(spots):
        low, high, lane = pieces_of(tile, keys)
        rows = slice(row, row + QT)
        span = slice(first, first + keys)
        local = slice(tile * QT, tile * QT + QT)
        grads = context_grad[head, rows, :]
        prob_grad = dot(grads, value[span, :], ROWS_T)
        row_dot = jnp.sum(
            grads.astype(F32) * context[rows, :].astype(F32), axis=1, keepdims=True
        )
        copy_of(head, index).wait()
        taken = (rest if first else prob)[head, local, :]
        score_grad = taken.astype(F32) * (prob_grad - row_dot)
        low_grad = score_grad.astype(BF)
        near_total[:, lane : lane + high - low] += score_grad[:, low:high]
        for side, (a, b) in enumerate(((0, low), (high, keys))):
            if b > a:
                far_total[side] += sum(score_grad[:, c : c + 128] for c in range(a, b, 128))
        parts_ref[0, :DH, rows] = dot(turned[:, span], low_grad, ROWS_T).astype(BF)
        value_part = dot(grads, taken, T_ROWS)
        key_part = dot(query[rows, :], low_grad, T_ROWS)
        if tile == 0:
            value_total[:, span] = value_part
            key_total[:, span] = key_part
        else:
            value_total[:, span] += value_part
            key_total[:, span] += key_part

    padded = jnp.concatenate(
        [near_total[...], jnp.zeros((QT, WIDE - near_total.shape[1]), F32)], axis=1
    )
    count = QT
    while count > 1:
        count //= 2
        padded = padded[:count] + pltpu.roll(padded[count:], WIDE - count, 1)
    line = pltpu.roll(padded, QT - 1, 1)
    lanes = lax.broadcasted_iota(jnp.int32, line.shape, 1)
    line = jnp.where(lanes == 0, jnp.sum(far_total[0]), line)
    line_ref[0] = jnp.where(lanes == WIDE - 1, jnp.sum(far_total[1]), line)

    parts_ref[0, DH : 2 * DH, :] = key_total[...].astype(BF)
    parts_ref[0, 2 * DH :, :] = value_total[...].astype(BF)

    @pl.when(head == 0)
    def _():
        normed_copy.wait()

    made = sum(
        dot(parts_ref[0, :, pl.ds(row, size)], normed[step])
        for step, row in enumerate(blocks)
    )
    for which in range(3):
        row = pl.multiple_of(which * whole + head * DH, DH)
        sums[pl.ds(row, DH), :] = made[which * DH : which * DH + DH]

    @pl.when(head == head_count - 1)
    def _():
        half = kept_ref.shape[0]
        for flip, out in enumerate((kept_ref, away_ref)):
            row = pl.multiple_of((bit ^ flip) * half, half)
            out[...] = sums[pl.ds(row, half), :].astype(out.dtype)


def attend_backward(place, grads, normed, output_weights, kept):
    packed, prob, rest, gathered = kept
    _, size, width = normed.shape
    head_count, total, _ = packed.shape
    rows = 4 * DH * head_count
    by_head = lambda *shape: pl.BlockSpec((1, *shape), lambda h: (h, *(0 for _ in shape)))
    whole = lambda *shape: pl.BlockSpec(shape, lambda h: tuple(0 for _ in shape))
    apart = pl.BlockSpec(memory_space=pl.ANY)
    return pl.pallas_call(
        backward_kernel,
        grid=(head_count,),
        out_shape=(
            struct((head_count, 3 * DH, total), BF),
            struct((head_count, 1, WIDE), F32),
            struct((rows // 2, width), F32),
            struct((rows // 2, width), BF),
        ),
        in_specs=[
            smem(),
            *(whole(size, width) for _ in range(4)),
            apart,
            whole(head_count * DH, width),
            by_head(total, 4 * DH),
            whole(total, head_count * DH),
            apart,
            apart,
        ],
        out_specs=(
            by_head(3 * DH, total),
            by_head(1, WIDE),
            whole(rows // 2, width),
            whole(rows // 2, width),
        ),
        scratch_shapes=[
            pltpu.VMEM(normed.shape, BF),
            pltpu.VMEM(prob.shape, BF),
            pltpu.VMEM(rest.shape, BF),
            *(pltpu.VMEM((total, DH), BF) for _ in range(4)),
            pltpu.VMEM((DH, total), BF),
            pltpu.VMEM((head_count, total, DH), BF),
            pltpu.VMEM((QT, QT + 2 * NEAR), F32),
            pltpu.VMEM((2, QT, 128), F32),
            pltpu.VMEM((DH, total), F32),
            pltpu.VMEM((DH, total), F32),
            pltpu.VMEM((rows, width), F32),
            pltpu.SemaphoreType.DMA((head_count, total // QT)),
            pltpu.SemaphoreType.DMA,
        ],
        compiler_params=params(56),
        cost_estimate=LONG_KERNEL,
        name="attend_backward",
    )(place, *grads, normed, output_weights, packed, gathered, prob, rest)


def normed_grad_kernel(
    place_ref,
    parts_ref,
    query_weight_ref,
    key_weight_ref,
    value_weight_ref,
    gain_ref,
    normed_ref,
    gain_two_ref,
    line_ref,
    away_ref,
    send_ref,
    keep_ref,
    rider_ref,
    loaded_ref,
):
    place = place_ref[0]
    size = normed_ref.shape[1]
    gain_grad = 0.0
    weights = (query_weight_ref, key_weight_ref, value_weight_ref)
    for step in range(4):
        row = pl.multiple_of((place ^ step) * size, size)
        made = 0.0
        for head in range(parts_ref.shape[0]):
            weight = jnp.concatenate([ref[head * DH : head * DH + DH, :] for ref in weights])
            made += dot(parts_ref[head, :, pl.ds(row, size)], weight, T_ROWS)
        out = send_ref if step & 1 else keep_ref
        out[step >> 1] = made.astype(BF)
        gain_grad += jnp.sum(made * normed_ref[step].astype(F32), axis=0, keepdims=True)
    rider_ref[...] = jnp.zeros_like(rider_ref)
    rider_ref[0:1, :] = gain_grad / gain_ref[...].astype(F32)
    rider_ref[1:2, :] = gain_two_ref[...]
    for head in range(line_ref.shape[0]):
        rider_ref[2 + head : 3 + head, :] = line_ref[head]
    half = away_ref.shape[0]
    loaded_ref[:half, :] = away_ref[...]
    loaded_ref[half:, :] = rider_ref[...].astype(BF)


def normed_grad(place, parts, weights, gain, normed, gain_two_grad, lines, away):
    _, size, width = normed.shape
    operands = (parts, *weights, gain, normed, gain_two_grad, lines, away)
    return call(
        normed_grad_kernel,
        "normed_grad",
        (
            struct((2, size, width), BF),
            struct((2, size, width), BF),
            struct((RIDER, width), F32),
            struct((away.shape[0] + RIDER, width), BF),
        ),
        (smem(), *operands),
        (place, *operands),
        cost=LONG_KERNEL,
    )


def inverse_root(values):
    return lax.rsqrt(jnp.mean(values * values, axis=-1, keepdims=True) + EPSILON)


def norm_input_grad(values, inverse, gains, upstream):
    scaled = upstream * gains
    projection = jnp.mean(scaled * values, axis=-1, keepdims=True)
    return inverse * scaled - values * (inverse * inverse * inverse) * projection


def middle_grad_kernel(
    cotangent_ref, middle_ref, own_ref, near_ref, far_ref, gain_ref, low_ref
):
    upstream = own_ref[...].astype(F32) + near_ref[...].astype(F32) + far_ref[...].astype(F32)
    values = middle_ref[...]
    grad = cotangent_ref[...].astype(F32) + norm_input_grad(
        values, inverse_root(values), gain_ref[...].astype(F32), upstream
    )
    low_ref[...] = grad.astype(BF)


def middle_rest_kernel(
    cotangent_ref, middle_ref, own_ref, near_ref, far_ref, gain_ref, grad_ref, gain_grad_ref
):
    upstream = own_ref[...].astype(F32) + near_ref[...].astype(F32) + far_ref[...].astype(F32)
    values = middle_ref[...]
    inverse = inverse_root(values)
    grad_ref[...] = cotangent_ref[...].astype(F32) + norm_input_grad(
        values, inverse, gain_ref[...].astype(F32), upstream
    )
    gain_grad_ref[...] = jnp.sum(upstream * values * inverse, axis=0, keepdims=True)


def make_middle_grad(cotangent, middle, sums, gain):
    operands = (cotangent, middle, *sums, gain)
    return call(
        middle_grad_kernel, "middle_grad", (struct(middle.shape, BF),), operands, operands
    )[0]


def make_middle_rest(cotangent, middle, sums, gain):
    operands = (cotangent, middle, *sums, gain)
    return call(
        middle_rest_kernel,
        "middle_rest",
        (struct(middle.shape, F32), struct((1, middle.shape[1]), F32)),
        operands,
        operands,
    )


def input_grad_kernel(input_ref, own_ref, near_ref, far_ref, gain_ref, middle_ref, out_ref):
    upstream = own_ref[0].astype(F32) + near_ref[0].astype(F32) + far_ref[...].astype(F32)
    values = input_ref[...].astype(F32)
    out_ref[...] = middle_ref[...] + norm_input_grad(
        values, inverse_root(values), gain_ref[...], upstream
    )


def make_input_grad(inputs, sums, gain, middle_grad):
    first = one((1, *inputs.shape))
    return call(
        input_grad_kernel,
        "input_grad",
        (struct(inputs.shape, F32),),
        (inputs, first, first, sums[2], gain, middle_grad),
        (inputs, *sums, gain, middle_grad),
    )[0]


def layer_output_kernel(middle_ref, own_ref, near_ref, far_ref, out_ref):
    own, near, far = (ref[...].astype(F32) for ref in (own_ref, near_ref, far_ref))
    out_ref[...] = (middle_ref[...] + (own + near + far)).astype(BF)


def make_layer_output(middle, sums):
    operands = (middle, *sums)
    return call(
        layer_output_kernel, "layer_output", (struct(middle.shape, BF),), operands, operands
    )[0]


def outer_kernel(weight_ref, *refs):
    hidden_refs, out_refs = refs[:4], refs[4:]
    for hidden, out in zip(hidden_refs, out_refs):
        out[...] = dot(hidden[...], weight_ref[...]).astype(BF)


def outer_product(hidden, weight):
    operands = (weight, *hidden)
    shape = struct((hidden[0].shape[0], weight.shape[1]), BF)
    return call(outer_kernel, "outer", (shape,) * 4, operands, operands, cost=LONG_KERNEL)


def after(values, *others):
    return lax.optimization_barrier((values, others))[0]


def across(values, axis, flip):
    count = lax.axis_size(axis)
    return lax.ppermute(values, axis, [(i, i ^ flip) for i in range(count)])


def over_core(values):
    return across(values, "tensor", 1)


def over_x(values):
    return across(values, "tensor", 2)


def usual():
    return lax.axis_size("dp") == 8


def split_kernel(place_ref, *refs):
    kept_ref, came_ref, *refs = refs
    riders, refs = refs[:-4], refs[-4:]
    own_ref, *away_refs = refs
    size = own_ref.shape[0]
    spot = place_ref[1] >> 1
    if riders:
        rider_ref, total_ref = riders
        half = kept_ref.shape[0]
        total_ref[...] = rider_ref[...] + came_ref[half:, :].astype(F32)
        for out in away_refs:
            out[size:, :] = total_ref[...].astype(BF)
    for flip, out in enumerate((own_ref, *away_refs)):
        rows = pl.ds(pl.multiple_of((spot ^ flip) * size, size), size)
        out[:size, :] = (kept_ref[rows, :] + came_ref[rows, :].astype(F32)).astype(out.dtype)


def four_kernel(own_ref, came0, came1, came2, *refs):
    *riders, out_ref = refs
    size = own_ref.shape[0]
    total = own_ref[...]
    for came in (came0, came1, came2):
        total += came[:size, :].astype(F32)
    out_ref[...] = total.astype(BF)
    if riders:
        rider_ref, sum_ref = riders
        total = rider_ref[...]
        for came in (came0, came1, came2):
            total += came[size:, :].astype(F32)
        sum_ref[...] = total


def pair_kernel(place_ref, own_ref, came_ref, out_ref):
    size = own_ref.shape[0]
    bit = (place_ref[1] >> 2) & 1
    for flip, ref in enumerate((own_ref, came_ref)):
        out_ref[pl.ds(pl.multiple_of((bit ^ flip) * size, size), size), :] = ref[...]


def half_kernel(place_ref, pair_ref, came_ref, out_ref):
    size = pair_ref.shape[0] // 2
    bit = (place_ref[1] >> 1) & 1
    for flip, ref in enumerate((pair_ref, came_ref)):
        for which in range(2):
            row = pl.multiple_of(((bit ^ flip) + 2 * which) * size, size)
            out_ref[pl.ds(row, size), :] = ref[which * size : which * size + size, :]


def join_kernel(place_ref, own_ref, came0, came1, came2, out_ref):
    size = own_ref.shape[0]
    spot = place_ref[1] >> 1
    for flip, ref in enumerate((own_ref, came0, came1, came2)):
        out_ref[pl.ds(pl.multiple_of((spot ^ flip) * size, size), size), :] = ref[...]


def whole_kernel(factor, pieces, place_ref, own_ref, came_ref, *refs):
    *out_refs, whole = refs
    part = own_ref.shape[0] // pieces
    bit = place_ref[1] & 1
    for flip, ref in enumerate((own_ref, came_ref)):
        for piece in range(pieces):
            row = pl.multiple_of((2 * piece + (bit ^ flip)) * part, part)
            whole[pl.ds(row, part), :] = ref[piece * part : piece * part + part, :]
    rows = whole.shape[0] // len(out_refs)
    for index, out in enumerate(out_refs):
        out[...] = whole[index * rows : index * rows + rows, :].astype(F32) * factor


def cut_kernel(place_ref, *refs):
    whole_refs, kept_ref, away_ref = refs[:-2], refs[-2], refs[-1]
    bit = place_ref[1] & 1
    half = whole_refs[0].shape[0] // 2
    for index, ref in enumerate(whole_refs):
        here = slice(index * half, index * half + half)
        for flip, out in enumerate((kept_ref, away_ref)):
            rows = pl.ds(pl.multiple_of((bit ^ flip) * half, half), half)
            out[here, :] = ref[rows, :].astype(out.dtype)


def cut(place, arrays):
    rows, width = arrays[0].shape
    shape = (len(arrays) * rows // 2, width)
    return call(
        cut_kernel, "cut", (struct(shape, F32), struct(shape, BF)), (smem(), *arrays), (place, *arrays)
    )


class Reduction:
    def __init__(self, name, place, pieces, kept, away, rider=None):
        self.name, self.place, self.pieces, self.rider = name, place, pieces, rider
        self.rows, self.width = 2 * kept.shape[0], kept.shape[1]
        self.stage = 0
        self.count = lax.axis_size("dp")
        self.halves = (kept, away[: kept.shape[0]])
        self.kept = kept
        if self.count == 8:
            self.came = across(away, "dp", 1)

    def step(self, *others):
        self.stage += 1
        if self.count != 8:
            if self.stage == 1 and self.rider is not None:
                self.rider = lax.psum(self.rider, "dp")
            return self.kept
        width = self.width
        name = f"{self.name}_{self.stage}"
        riders = () if self.rider is None else (self.rider,)
        also = tuple(struct(item.shape, F32) for item in riders)
        if self.stage == 1:
            size = self.rows // 8
            far = size + sum(item.shape[0] for item in riders)
            operands = (self.kept, after(self.came, *others), *riders)
            *riders, own, a, b, c = call(
                split_kernel,
                name,
                (*also, struct((size, width), F32), *(struct((far, width), BF) for _ in range(3))),
                (smem(), *operands),
                (self.place, *operands),
                cost=FREE if self.rider is None else LONG_KERNEL,
            )
            self.kept = own
            self.came = [across(item, "dp", 2 * flip) for flip, item in enumerate((a, b, c), 1)]
            self.rider = riders[0] if riders else None
            return own
        if self.stage == 2:
            operands = (self.kept, *after(self.came, *others), *riders)
            *riders, low = call(
                four_kernel, name, (*also, struct(self.kept.shape, BF)), operands, operands
            )
            self.kept = low
            if riders:
                self.came = [across(low, "dp", 2 * flip) for flip in range(1, 4)]
                self.rider = riders[0]
            else:
                self.came = across(low, "dp", 4)
            return low
        if self.rider is None:
            flip, kernel = {3: (2, pair_kernel), 4: (1, half_kernel)}[self.stage]
            operands = (self.kept, after(self.came, *others))
            rows = 2 * self.kept.shape[0]
            self.kept = call(
                kernel,
                name,
                (struct((rows, width), BF),),
                (smem(), *operands),
                (self.place, *operands),
                cost=LONG_KERNEL if self.stage == 3 else FREE,
            )[0]
            self.came = across(self.kept, "dp", flip)
            return self.kept
        if self.stage == 3:
            operands = (self.kept, *after(self.came, *others))
            half = call(
                join_kernel,
                name,
                (struct((self.rows // 2, width), BF),),
                (smem(), *operands),
                (self.place, *operands),
            )[0]
            self.kept = half
            self.came = across(half, "dp", 1)
            return half
        raise ValueError("over")

    def finish(self, factor, count, *others):
        own, came = self.kept, self.came if self.count == 8 else None
        if self.count != 8:
            kept, away = self.halves
            bit = lax.axis_index("dp") & 1
            away = away.astype(F32)
            first = jnp.where(bit == 0, kept, away)
            second = jnp.where(bit == 0, away, kept)
            total = sum_over_dp(jnp.concatenate([first, second])).astype(BF)
            half = kept.shape[0]
            own = lax.dynamic_slice_in_dim(total, bit * half, half)
            came = lax.dynamic_slice_in_dim(total, (1 - bit) * half, half)
        operands = (own, after(came, *others))
        width = self.width
        return call(
            functools.partial(whole_kernel, factor, self.pieces),
            self.name,
            (struct((self.rows // count, width), F32),) * count,
            (smem(), *operands),
            (self.place, *operands),
            (pltpu.VMEM((self.rows, width), BF),),
        )


def sum_over_dp(values):
    count = lax.axis_size("dp")
    if count & (count - 1) or values.shape[0] % count:
        return lax.psum(values, "dp")
    index = lax.axis_index("dp")
    bits = count.bit_length() - 1
    for bit in range(bits):
        half = values.shape[0] // 2
        mine = (index >> bit) & 1
        keep = lax.dynamic_slice_in_dim(values, mine * half, half)
        away = lax.dynamic_slice_in_dim(values, (1 - mine) * half, half)
        values = keep + across(away.astype(BF), "dp", 1 << bit).astype(F32)
    values = values.astype(BF)
    for bit in reversed(range(bits)):
        mine = (index >> bit) & 1
        came = across(values, "dp", 1 << bit)
        first = jnp.where(mine == 0, values, came)
        second = jnp.where(mine == 0, came, values)
        values = jnp.concatenate([first, second])
    return values.astype(F32)


ROOT = 0.7978845608028654
CUBE = 0.044715


def gate(value):
    square = value * value
    tanh = jnp.tanh(ROOT * value * (1.0 + CUBE * square))
    half = 0.5 * (1.0 + tanh)
    slope = half + 0.5 * ROOT * value * (1.0 - tanh * tanh) * (1.0 + 3.0 * CUBE * square)
    return value * half, slope


def body(
    inputs,
    segments,
    first_gain,
    query_weight,
    lookup_projection,
    value_weight,
    output_weight,
    bucket_bias_table,
    second_gain,
    inner_weight,
    outer_weight,
    cotangent,
):
    total = segments.shape[0]
    size, width = inputs.shape
    head_count = query_weight.shape[1] // DH
    factor = float(total * lax.axis_size("dp")) ** (-0.5)

    far, near_block = over_x(inputs), over_core(inputs)
    place = jnp.stack([lax.axis_index("tensor"), lax.axis_index("dp")]).astype(jnp.int32)
    gain_one = first_gain.astype(F32)
    gain_two = second_gain.astype(F32)
    gain_row = gain_one.reshape(1, -1)
    table = bucket_bias_table.astype(F32)
    weights = (query_weight.T, lookup_projection.T, value_weight.T)
    key_segment = segments[LONG:].reshape(1, -1)
    near, row_segment = near_bias(table, key_segment)
    norm_input = inputs.astype(F32)
    inverse_one = inverse_root(norm_input)
    far = after(far, near, row_segment, place, gain_row, inverse_one)
    blocks = (inputs, near_block, far, over_core(far))
    cot_far = over_x(after(cotangent, far))
    cot_near = over_core(after(cotangent, far))

    *kept, normed_one, send, keep, gathered = attend_forward(
        place, table, blocks, gain_row, weights, near, row_segment, key_segment, output_weight
    )
    kept.append(gathered)
    cot_far = after(cot_far, keep)
    send = after(send, cot_far)
    near_sums = [None, over_core(send[1])]
    near_sums[0] = over_core(after(send[0], near_sums[1]))
    outward = (keep[1].astype(F32) + near_sums[1].astype(F32)).astype(BF)
    far_sum = over_x(outward)
    cot_far = after(cot_far, outward)
    cotangents = (cotangent, cot_near, cot_far, over_core(cot_far))
    hidden_grads = {}
    for step in (2, 3):
        hidden_grads[step] = dot(cotangents[step], outer_weight, ROWS_T)
    far_sum = after(far_sum, hidden_grads)

    middle = norm_input + (
        keep[0].astype(F32) + near_sums[0].astype(F32) + far_sum.astype(F32)
    )
    inverse_two = inverse_root(middle)
    low = (middle * inverse_two * gain_two).astype(BF)
    normed_two = [low, over_core(low), over_x(low)]

    hidden, inner_grads, second = {}, {}, {}

    def feed(step):
        values, slope = gate(dot(normed_two[step], inner_weight))
        hidden[step] = values.astype(BF)
        if step not in hidden_grads:
            hidden_grads[step] = dot(cotangents[step], outer_weight, ROWS_T)
        inner_grads[step] = (hidden_grads[step] * slope).astype(BF)
        second[step] = dot(inner_grads[step], inner_weight, ROWS_T).astype(BF)

    def weight_grads(steps):
        outer = sum(dot(hidden[step], cotangents[step], T_ROWS) for step in steps)
        inner = sum(dot(normed_two[step], inner_grads[step], T_ROWS) for step in steps)
        return outer, inner

    feed(0)
    feed(1)
    second_near_one = over_core(second[1])
    first_grads = weight_grads((0, 1))
    normed_two[2] = after(normed_two[2], second, first_grads)
    normed_two.append(over_core(normed_two[2]))
    feed(2)
    normed_two[3] = after(normed_two[3], second[2])
    feed(3)
    second_near_three = over_core(second[3])
    outward = (second[2].astype(F32) + second_near_three.astype(F32)).astype(BF)
    second_far = over_x(outward)

    far_grads = after((hidden[2], hidden[3], inner_grads[2], inner_grads[3]), outward)
    hidden[2], hidden[3], inner_grads[2], inner_grads[3] = far_grads
    outer_grad, inner_grad = (
        left + right for left, right in zip(first_grads, weight_grads((2, 3)))
    )
    feed_sum = Reduction("feed_sum", place, 2, *cut(place, (outer_grad, inner_grad)))

    second_far = after(second_far, feed_sum.kept)
    sums = (second[0], second_near_one, second_far)
    low = make_middle_grad(cotangent, middle, sums, gain_two.reshape(1, -1))
    grads = [low, over_core(low), over_x(low)]
    outer_parts = outer_product(after([hidden[step] for step in range(4)], low), outer_weight)
    outer_near = [over_core(outer_parts[1]), over_core(outer_parts[3])]
    middle_grad, gain_two_grad = make_middle_rest(
        cotangent, middle, after(sums, outer_parts), gain_two.reshape(1, -1)
    )
    grads[2] = after(grads[2], outer_parts, middle_grad)
    grads.append(over_core(grads[2]))
    outward = outer_parts[2].astype(F32) + outer_near[1].astype(F32)
    outward = outward.astype(BF)
    mark = feed_sum.step(grads[3], outward)

    parts, lines, held, away = attend_backward(
        place, after(grads, mark), normed_one, output_weight, kept
    )
    outer_far = over_x(after(outward, held))
    mark = feed_sum.step(held)
    send, keep, rider, loaded = normed_grad(
        place, after(parts, mark), weights, gain_row, normed_one, gain_two_grad, lines, away
    )
    attention_sum = Reduction("attention_sum", place, 1, held, loaded, rider)
    layer_output = make_layer_output(
        middle, (outer_parts[0], outer_near[0], after(outer_far, keep))
    )
    first_near = over_core(send)
    mark = feed_sum.step(layer_output)
    mark = attention_sum.step(mark)
    outward = keep[1].astype(F32) + after(first_near[1], mark).astype(F32)
    outward = outward.astype(BF)
    first_far = over_x(outward)
    mark = feed_sum.step(outward)
    input_grad = make_input_grad(
        inputs, (keep, first_near, after(first_far, mark)), gain_row, middle_grad
    )
    mark = attention_sum.step(input_grad)
    small = attention_sum.rider
    gains = small[:8] + over_core(small[:8])
    mark = attention_sum.step(mark)
    outer_weight_grad, inner_weight_grad = feed_sum.finish(factor, 2, mark)
    gain_grads = (gains + over_x(gains))[:2]
    query_grad, key_grad, value_grad, output_weight_grad = attention_sum.finish(
        factor, 4, inner_weight_grad
    )

    slots = jnp.arange(table.shape[0], dtype=jnp.int32)
    offsets = jnp.arange(WIDE, dtype=jnp.int32) - (QT + NEAR - 1)
    chosen = buckets_of(offsets)[None, :] == slots[:, None]
    table_grad = jnp.sum(
        jnp.where(chosen[:, None, :], small[2 : 2 + head_count][None], 0.0), axis=2
    )
    return (
        layer_output,
        input_grad,
        query_grad.T,
        key_grad.T,
        value_grad.T,
        output_weight_grad,
        table_grad * factor,
        inner_weight_grad,
        outer_weight_grad,
        gain_grads * factor,
    )


def solution(mesh):
    return jax.shard_map(
        body,
        mesh=mesh,
        in_specs=(
            P(("dp", "tensor"), None),
            P("dp"),
            P(),
            P(None, "tensor"),
            P(None, "tensor"),
            P(None, "tensor"),
            P("tensor", None),
            P(None, "tensor"),
            P(),
            P(None, "tensor"),
            P("tensor", None),
            P(("dp", "tensor"), None),
        ),
        out_specs=(
            P(("dp", "tensor"), None),
            P(("dp", "tensor"), None),
            P(None, "tensor"),
            P(None, "tensor"),
            P(None, "tensor"),
            P("tensor", None),
            P(None, "tensor"),
            P(None, "tensor"),
            P("tensor", None),
            P(),
        ),
        check_vma=False,
    )
```
